512 devices in a mesh: depth: 8 (over y), tile: 64 (over x, z, core).
Axes of the slice: x: 4, y: 8, z: 8, core: 2. Of those that a mesh axis runs over, the one named last changes fastest.
Arguments:
- transmission: float32 [8, 64, 2, 256, 256], P('depth', 'tile'), may hold values from -0.6 to 1.6, as said below
- probe_modes: float32 [4, 2, 128, 128], replicated, may hold values from -3 to 3
- propagator_phase: float32 [128, 128], replicated, may hold values from -3.140625 to 3.140625
- measured: float32 [64, 4, 128, 128], P('tile'), may hold values from 0 to 2
- counts: int32 [64], P('tile'), may hold values from 2 to 4, as said below
- offsets: int32 [64, 4, 2], P('tile'), may hold values from 0 to 384, as said below
Outputs:
- object_grad: float32 [8, 64, 2, 256, 256], P('depth', 'tile')
The draws below stay inside these ranges and needn't reach their ends.
Inputs may be any that keep to these rules, and one draw needn't show every extreme that they name: `counts`: each tile has 2 to 4 positions, in its first slots; some tile has exactly 4. `offsets`: rows run up to 384, columns up to 384. In every tile, slot 0's patch reaches into the upper and left margins and slot 1's into the lower and right margins. `transmission`: real parts lie near 1 and imaginary parts near 0.
All inputs are finite; a program needn't handle non-finite values.
Results may differ from the reference program's by a relative error of at most 0.014.
Values may be sent and summed in bfloat16 or wider, within the bound.
A program may use at most 64 MiB of HBM per device.

```python
import math
import jax
import jax.numpy as jnp
from jax import lax

PN = 128
MODES = 4
PMAX = 4
TCOLS = 4
TR = 256
TC = 256
TILES = 64
SLICES = 8


def draw_counts(key, part):
    key_count, key_pick = jax.random.split(key)
    values = jax.random.randint(key_count, (TILES,), 2, PMAX + 1)
    chosen = jax.random.randint(key_pick, (), 0, TILES)
    return jnp.where(jnp.arange(TILES) == chosen, PMAX, values).astype(jnp.int32)


def draw_offsets(key, part):
    key_list = jax.random.split(jax.random.fold_in(key, 11), 7)
    row_starts = jax.random.randint(key_list[0], (TILES, PMAX), 0, TR + PN + 1)
    col_starts = jax.random.randint(key_list[1], (TILES, PMAX), 0, TC + PN + 1)
    top_rows = jax.random.randint(key_list[2], (TILES,), 0, PN // 2)
    left_cols = jax.random.randint(key_list[3], (TILES,), 0, PN // 2)
    low_rows = jax.random.randint(key_list[4], (TILES,), TR + PN // 2, TR + PN + 1)
    right_cols = jax.random.randint(key_list[5], (TILES,), TC + PN // 2, TC + PN + 1)
    chosen = jax.random.randint(key_list[6], (), 0, TILES)
    tile_ids = jnp.arange(TILES)
    top_rows = jnp.where(tile_ids == chosen, 0, top_rows)
    left_cols = jnp.where(tile_ids == chosen, 0, left_cols)
    low_rows = jnp.where(tile_ids == chosen, TR + PN, low_rows)
    right_cols = jnp.where(tile_ids == chosen, TC + PN, right_cols)
    row_starts = row_starts.at[:, 0].set(top_rows).at[:, 1].set(low_rows)
    col_starts = col_starts.at[:, 0].set(left_cols).at[:, 1].set(right_cols)
    return jnp.stack([row_starts, col_starts], axis=-1).astype(jnp.int32)


def draw_transmission(key, part):
    key_real, key_imag = jax.random.split(jax.random.fold_in(key, 23))
    grid_shape = (SLICES, TILES, TR, TC)
    real_part = 1.0 + 0.15 * jax.random.truncated_normal(key_real, -4.0, 4.0, grid_shape, jnp.float32)
    imag_part = 0.15 * jax.random.truncated_normal(key_imag, -4.0, 4.0, grid_shape, jnp.float32)
    return jnp.stack([real_part, imag_part], axis=2).astype(jnp.float32)


def level_of(stream_key, shape, cuts, low, largest):
    def one(axis_at, shards_of):
        steps = jax.random.uniform(jax.random.fold_in(jax.random.fold_in(stream_key, 6), axis_at), (shards_of,), jnp.float32, low / len(cuts), largest / len(cuts))
        return jnp.repeat(jnp.exp(steps), shape[axis_at] // shards_of).reshape((-1,) + (1,) * (len(shape) - axis_at - 1))

    factor_of = one(*cuts[0])
    for cut in cuts[1:]:
        factor_of = factor_of * one(*cut)
    return factor_of


def gaussian(own_key, shape, width, reach, kind=jnp.bfloat16):
    entries = width * jax.random.normal(own_key, shape, jnp.float32)
    return jnp.clip(entries, min=-reach, max=reach).astype(kind)


def setup_inputs(seed: int = 0) -> dict:
    seeds = jax.random.split(jax.random.key(seed), 7)
    transmission = draw_transmission(jax.random.fold_in(seeds[6], 71), 0)
    probe_modes = gaussian(seeds[1], (MODES, 2, PN, PN), 0.5, 3.0, jnp.float32)
    propagator_phase = jnp.clip(jax.random.uniform(seeds[2], (PN, PN), jnp.float32, -3.140625, 3.140625), -3.140625, 3.140625)
    measured = jnp.clip(2.0 * jax.random.uniform(seeds[3], (TILES, PMAX, PN, PN), jnp.float32) ** level_of(seeds[3], (TILES, PMAX, PN, PN), ((0, 64),), -0.2, 0.2), 0.0, 2.0)
    counts = draw_counts(jax.random.fold_in(seeds[6], 71), 0)
    offsets = draw_offsets(jax.random.fold_in(seeds[6], 71), 0)
    return {"transmission": transmission, "probe_modes": probe_modes, "propagator_phase": propagator_phase, "measured": measured, "counts": counts, "offsets": offsets}


highest = lax.Precision.HIGHEST

def dft_pair(probe_side):
    index_row = jnp.arange(probe_side, dtype=jnp.int32)
    product = index_row[:, None] * index_row[None, :] % probe_side
    angle_grid = product.astype(jnp.float32) * (-2.0 * math.pi / probe_side)
    norm_factor = 1.0 / math.sqrt(probe_side)
    return (jnp.cos(angle_grid) * norm_factor, jnp.sin(angle_grid) * norm_factor)

def transform(wave_field, pair_table, inverse):
    real_t = pair_table[0]
    imag_t = -pair_table[1] if inverse else pair_table[1]
    wave_re = wave_field[:, 0]
    wave_im = wave_field[:, 1]
    left_re = jnp.einsum('jk,bkl->bjl', real_t, wave_re, precision=highest) - jnp.einsum('jk,bkl->bjl', imag_t, wave_im, precision=highest)
    left_im = jnp.einsum('jk,bkl->bjl', real_t, wave_im, precision=highest) + jnp.einsum('jk,bkl->bjl', imag_t, wave_re, precision=highest)
    out_re = jnp.einsum('bjk,kl->bjl', left_re, real_t, precision=highest) - jnp.einsum('bjk,kl->bjl', left_im, imag_t, precision=highest)
    out_im = jnp.einsum('bjk,kl->bjl', left_re, imag_t, precision=highest) + jnp.einsum('bjk,kl->bjl', left_im, real_t, precision=highest)
    return jnp.stack([out_re, out_im], axis=1)

def complex_mul(factor_one, factor_two):
    one_re = factor_one[..., 0, :, :]
    one_im = factor_one[..., 1, :, :]
    two_re = factor_two[..., 0, :, :]
    two_im = factor_two[..., 1, :, :]
    return jnp.stack([one_re * two_re - one_im * two_im, one_re * two_im + one_im * two_re], axis=-3)

def conj_mul(factor_one, factor_two):
    one_re = factor_one[..., 0, :, :]
    one_im = factor_one[..., 1, :, :]
    two_re = factor_two[..., 0, :, :]
    two_im = factor_two[..., 1, :, :]
    return jnp.stack([one_re * two_re + one_im * two_im, one_im * two_re - one_re * two_im], axis=-3)

def propagate(wave_field, kernel, pair_table):
    spectrum = complex_mul(transform(wave_field, pair_table, False), kernel)
    return transform(spectrum, pair_table, True)

def adjoint(wave_field, kernel, pair_table):
    spectrum = conj_mul(transform(wave_field, pair_table, False), kernel)
    return transform(spectrum, pair_table, True)

def to_half(wave_field):
    return lax.optimization_barrier(wave_field.astype(jnp.bfloat16)).astype(jnp.float32)

def reference(transmission, probe_modes, propagator_phase, measured, counts, offsets):
    probe_side = PN
    pair_table = dft_pair(probe_side)
    kernel = jnp.stack([jnp.cos(propagator_phase), jnp.sin(propagator_phase)])
    grid_rows = TILES // TCOLS
    whole_object = transmission.reshape(SLICES, grid_rows, TCOLS, 2, TR, TC).transpose(0, 3, 1, 4, 2, 5)
    whole_object = whole_object.reshape(SLICES, 2, grid_rows * TR, TCOLS * TC)
    padded = jnp.pad(whole_object, ((0, 0), (0, 0), (probe_side, probe_side), (probe_side, probe_side)))
    probe_items = jnp.tile(probe_modes, (PMAX, 1, 1, 1))
    anchor = jnp.zeros((), jnp.int32)

    def one_tile(grad_pad, inputs):
        tile_index, tile_count, tile_offsets, tile_measured = inputs
        base_row = (tile_index // TCOLS * TR).astype(jnp.int32)
        base_col = (tile_index % TCOLS * TC).astype(jnp.int32)

        def cut_patch(row_start, col_start):
            return lax.dynamic_slice(padded, (anchor, anchor, base_row + row_start, base_col + col_start), (SLICES, 2, probe_side, probe_side))
        patches = jax.vmap(cut_patch)(tile_offsets[:, 0], tile_offsets[:, 1])
        screens = jnp.repeat(patches, MODES, axis=0)
        valid_slots = (jnp.arange(PMAX, dtype=jnp.int32) < tile_count).astype(jnp.float32)
        wave_now = probe_items
        entering_list = []
        for slice_index in range(SLICES):
            entering_list.append(wave_now)
            wave_now = propagate(complex_mul(screens[:, slice_index], wave_now), kernel, pair_table)
            if slice_index < SLICES - 1:
                wave_now = to_half(wave_now)
        far = transform(wave_now, pair_table, False)
        grouped = far.reshape(PMAX, MODES, 2, probe_side, probe_side)
        intensity = lax.optimization_barrier(jnp.sum(grouped[:, :, 0] ** 2 + grouped[:, :, 1] ** 2, axis=1))
        weight = 4.0 * valid_slots[:, None, None] * (intensity - tile_measured)
        scaled = grouped * weight[:, None, None, :, :]
        back_wave = transform(scaled.reshape(PMAX * MODES, 2, probe_side, probe_side), pair_table, True)
        grad_list = [None] * SLICES
        for slice_index in range(SLICES - 1, -1, -1):
            spread = adjoint(back_wave, kernel, pair_table)
            item_grad = conj_mul(spread, entering_list[slice_index])
            grad_list[slice_index] = lax.optimization_barrier(jnp.sum(item_grad.reshape(PMAX, MODES, 2, probe_side, probe_side), axis=1))
            if slice_index > 0:
                back_wave = to_half(conj_mul(spread, screens[:, slice_index]))
        patch_grad = jnp.stack(grad_list, axis=1)
        for slot_index in range(PMAX):
            corner = (anchor, anchor, base_row + tile_offsets[slot_index, 0], base_col + tile_offsets[slot_index, 1])
            window = lax.dynamic_slice(grad_pad, corner, (SLICES, 2, probe_side, probe_side))
            grad_pad = lax.dynamic_update_slice(grad_pad, window + patch_grad[slot_index], corner)
        return (grad_pad, None)
    start_grad = jnp.zeros(padded.shape, jnp.float32)
    grad_pad, unused = lax.scan(one_tile, start_grad, (jnp.arange(TILES, dtype=jnp.int32), counts, offsets, measured))
    interior = grad_pad[:, :, probe_side:-probe_side, probe_side:-probe_side]
    interior = interior.reshape(SLICES, 2, grid_rows, TR, TCOLS, TC).transpose(0, 2, 4, 1, 3, 5)
    return interior.reshape(SLICES, TILES, 2, TR, TC)
```

```python
import functools
import math

import jax
import jax.numpy as jnp
import ml_dtypes
import numpy as np
from jax import lax
from jax.experimental import pallas as pl
from jax.experimental.pallas import tpu as pltpu
from jax.sharding import PartitionSpec as P

TCOLS = 4
N = 128
SCALE = 1.6657
FMODE = 3
BMODE = 1
MESH = pl.DeviceIdType.MESH


def dft_tables():
    k = np.arange(N)
    angle = -2 * np.pi * ((k[:, None] * k[None, :]) % N) / N
    re, im = np.cos(angle) * SCALE, np.sin(angle) * SCALE
    g = np.block([[re, -im], [im, re]])
    both = np.stack([g, g.T]).astype(np.float32)
    high = both.astype(ml_dtypes.bfloat16)
    low = (both - high.astype(np.float32)).astype(ml_dtypes.bfloat16)
    values = np.cos(2 * np.pi * np.arange(N // 4 + 1) / N) * SCALE
    rounded = values.astype(np.float32).astype(ml_dtypes.bfloat16).astype(np.float64)
    gain = float(rounded @ values) / float(values @ values)
    return np.stack([high, low]), gain


TABLES, GAIN = dft_tables()
UNIT = 1.0 / (math.sqrt(N) * SCALE)
UNIT_F = UNIT / GAIN if FMODE == 1 else UNIT
UNIT_B = UNIT / GAIN if BMODE == 1 else UNIT


def blocks(y):
    return y[:N, :N], y[:N, N:], y[N:, :N], y[N:, N:]


def square(a, b, c, d):
    return jnp.concatenate([jnp.concatenate([a, b], 1), jnp.concatenate([c, d], 1)], 0)


def swap(y):
    a, b, c, d = blocks(y)
    return square(a, c, b, d)


def split(x):
    high = x.astype(jnp.bfloat16)
    return high, (x - high.astype(jnp.float32)).astype(jnp.bfloat16)


def dot(a, b):
    return jnp.dot(a, b, preferred_element_type=jnp.float32)


def left(tab, which, x, mode):
    gh = tab[0, which]
    if mode == 1:
        return dot(gh, x.astype(jnp.bfloat16))
    gl = tab[1, which]
    h, l = split(x)
    return dot(jnp.concatenate([gh, gh, gl], 1), jnp.concatenate([h, l, h], 0))


def right(tab, which, x, mode):
    gh = tab[0, which]
    if mode == 1:
        return dot(x.astype(jnp.bfloat16), gh)
    gl = tab[1, which]
    h, l = split(x)
    return dot(jnp.concatenate([h, l, h], 1), jnp.concatenate([gh, gh, gl], 0))


def mul_columns(x, sr, si):
    r1, r2, i1, i2 = blocks(x)
    return square(sr * r1 - si * i1, sr * r2 - si * i2, sr * i1 + si * r1, sr * i2 + si * r2)


def mul_rows(x, sr, si):
    r1, i1, r2, i2 = blocks(x)
    return square(sr * r1 - si * i1, sr * i1 + si * r1, sr * r2 - si * i2, sr * i2 + si * r2)


def propagate(tab, xs, hr, hi, mode):
    xs = [swap(left(tab, 0, x, mode)) for x in xs]
    xs = [mul_rows(right(tab, 1, x, mode), hr, hi) for x in xs]
    xs = [swap(right(tab, 0, x, mode)) for x in xs]
    return [left(tab, 1, x, mode) for x in xs]


def kernel(
    depth, tiles, slots, pairs,
    own, probe, phase, measured, counts, offsets, tab,
    out,
    frame, rows_of, cols_of, rows_back, cols_back, cropped, patch, screens, wave, prop, gout, gin, gcols, gframe,
    hout, hin, vout, vin,
    v_send, v_recv, h_send, h_recv, p_send, p_recv, g_send, g_recv, fh_send, fh_recv, fv_send, fv_recv,
):
    y = lax.axis_index("depth")
    t = lax.axis_index("tile")
    core = lax.rem(t, 2)
    col = lax.rem(t, TCOLS)
    row = lax.div(t, TCOLS)
    has_up, has_down = row > 0, row < tiles // TCOLS - 1
    has_left, has_right = col > 0, col < TCOLS - 1
    bf = jnp.bfloat16
    f32 = jnp.float32

    barrier = pltpu.get_barrier_semaphore()
    around = ((has_up, -TCOLS), (has_down, TCOLS), (has_left, -1), (has_right, 1))
    for there, by in around:
        @pl.when(there)
        def _():
            pl.semaphore_signal(barrier, inc=1, device_id=(y, t + by), device_id_type=MESH)
    for k in range(1, depth):
        pl.semaphore_signal(barrier, inc=1, device_id=(lax.rem(y + k, depth), t), device_id_type=MESH)

    for ri in range(2):
        for cb in range(2):
            frame[ri, 1 + cb, N : 3 * N] = own[ri, :, cb * N : (cb + 1) * N].astype(bf)
    zero = jnp.zeros((2, 2, N, N), bf)

    @pl.when(jnp.logical_not(has_up))
    def _():
        frame[:, 1:3, 0:N] = zero

    @pl.when(jnp.logical_not(has_down))
    def _():
        frame[:, 1:3, 3 * N : 4 * N] = zero

    @pl.when(jnp.logical_not(has_left))
    def _():
        frame[:, 0] = jnp.zeros((2, 4 * N, N), bf)

    @pl.when(jnp.logical_not(has_right))
    def _():
        frame[:, 3] = jnp.zeros((2, 4 * N, N), bf)

    pl.semaphore_wait(
        barrier,
        depth - 1 + sum(there.astype(jnp.int32) for there, _ in around),
    )

    def halo_down():
        return pltpu.make_async_remote_copy(
            src_ref=frame.at[:, 1:3, 2 * N : 3 * N], dst_ref=frame.at[:, 1:3, 0:N],
            send_sem=v_send.at[0], recv_sem=v_recv.at[0], device_id=(y, t + TCOLS), device_id_type=MESH)

    def halo_up():
        return pltpu.make_async_remote_copy(
            src_ref=frame.at[:, 1:3, N : 2 * N], dst_ref=frame.at[:, 1:3, 3 * N : 4 * N],
            send_sem=v_send.at[1], recv_sem=v_recv.at[1], device_id=(y, t - TCOLS), device_id_type=MESH)

    pieces = ((0, N), (3 * N, 4 * N), (N, 3 * N))

    def halo_right(k):
        lo, hi = pieces[k]
        return pltpu.make_async_remote_copy(
            src_ref=frame.at[:, 2, lo:hi], dst_ref=frame.at[:, 0, lo:hi],
            send_sem=h_send.at[0, k], recv_sem=h_recv.at[0, k], device_id=(y, t + 1), device_id_type=MESH)

    def halo_left(k):
        lo, hi = pieces[k]
        return pltpu.make_async_remote_copy(
            src_ref=frame.at[:, 1, lo:hi], dst_ref=frame.at[:, 3, lo:hi],
            send_sem=h_send.at[1, k], recv_sem=h_recv.at[1, k], device_id=(y, t - 1), device_id_type=MESH)

    def sideways(k):
        @pl.when(has_right)
        def _():
            halo_right(k).start()

        @pl.when(has_left)
        def _():
            halo_left(k).start()

    @pl.when(has_down)
    def _():
        halo_down().start()

    @pl.when(has_up)
    def _():
        halo_up().start()

    sideways(2)

    for p in range(slots):
        r, c = offsets[2 * p], offsets[2 * p + 1]
        wide = lax.broadcasted_iota(jnp.int32, (N, 4 * N), 1) - lax.broadcasted_iota(jnp.int32, (N, 4 * N), 0)
        tall = lax.broadcasted_iota(jnp.int32, (4 * N, N), 0) - lax.broadcasted_iota(jnp.int32, (4 * N, N), 1)
        rows_of[p * N : (p + 1) * N] = jnp.where(wide == r, 1.0, 0.0).astype(bf)
        cols_back[p] = jnp.where(wide == c, 1.0, 0.0).astype(bf)
        rows_back[:, p * N : (p + 1) * N] = jnp.where(tall == r, 1.0, 0.0).astype(bf)
        cols_of[p] = jnp.where(tall == c, 1.0, 0.0).astype(bf)
    angle = phase[...]
    prop[0] = jnp.cos(angle)
    prop[1] = jnp.sin(angle)
    for q in range(pairs):
        wave[0, q] = square(probe[2 * q, 0], probe[2 * q + 1, 0], probe[2 * q, 1], probe[2 * q + 1, 1])

    @pl.when(has_up)
    def _():
        halo_down().wait_recv()

    sideways(0)

    @pl.when(has_down)
    def _():
        halo_up().wait_recv()

    sideways(1)

    def crop_rows(cb):
        got = dot(rows_of[...], jnp.concatenate([frame[0, cb], frame[1, cb]], 1)).astype(bf)
        for p in range(slots):
            for ri in range(2):
                cropped[p, ri * N : (ri + 1) * N, cb * N : (cb + 1) * N] = got[p * N : (p + 1) * N, ri * N : (ri + 1) * N]

    crop_rows(1)
    crop_rows(2)
    for k in (2, 0, 1):
        @pl.when(has_left)
        def _():
            halo_right(k).wait_recv()

        @pl.when(has_right)
        def _():
            halo_left(k).wait_recv()

    crop_rows(0)
    crop_rows(3)

    def patch_copy(p, s):
        return pltpu.make_async_remote_copy(
            src_ref=patch.at[p], dst_ref=screens.at[s],
            send_sem=p_send.at[p], recv_sem=p_recv.at[s], device_id=(2 * p + core, t), device_id_type=MESH)

    for p in range(slots):
        got = dot(cropped[p], cols_of[p]).astype(bf)
        patch[p, 0] = got[:N]
        patch[p, 1] = got[N:]

        @pl.when(y != 2 * p + core)
        def _():
            patch_copy(p, y).start()

        @pl.when(y == 2 * p + core)
        def _():
            screens[y] = patch[p]

    mine = lax.div(y, 2)

    def grad_copy(s, p):
        return pltpu.make_async_remote_copy(
            src_ref=gout.at[s], dst_ref=gin.at[p],
            send_sem=g_send.at[s], recv_sem=g_recv.at[p], device_id=(s, t), device_id_type=MESH)

    @pl.when(lax.rem(y, 2) == core)
    def _():
        def screen(s):
            return screens[s, 0].astype(f32), screens[s, 1].astype(f32)

        def arrive(s):
            @pl.when(y != s)
            def _():
                patch_copy(0, s).wait_recv()

        def forward(s, carry):
            arrive(s)
            sr, si = screen(s)
            xs = [mul_columns(wave[s, q], sr, si) for q in range(pairs)]
            xs = propagate(tab, xs, prop[0] * UNIT_F**4, prop[1] * UNIT_F**4, FMODE)
            for q in range(pairs):
                wave[s + 1, q] = xs[q]
            return carry

        lax.fori_loop(0, depth - 1, forward, 0)
        arrive(depth - 1)
        sr, si = screen(depth - 1)
        xs = [mul_columns(wave[depth - 1, q], sr, si) for q in range(pairs)]
        xs = [swap(left(tab, 0, x, FMODE)) for x in xs]
        xs = [mul_rows(right(tab, 1, x, FMODE), prop[0] * UNIT_F**2, prop[1] * UNIT_F**2) for x in xs]
        intensity = jnp.zeros((N, N), f32)
        for x in xs:
            for part in blocks(x):
                intensity = intensity + part * part
        valid = jnp.where(mine < counts[0], 4.0 * UNIT_B**2, 0.0)
        weight = (intensity - measured[mine]) * valid
        xs = [mul_rows(x, prop[0] * weight, -prop[1] * weight) for x in xs]
        xs = [swap(right(tab, 0, x, BMODE)) for x in xs]
        us = [left(tab, 1, x, BMODE) for x in xs]

        def leave(s, us):
            gr = jnp.zeros((N, N), f32)
            gi = jnp.zeros((N, N), f32)
            for q in range(pairs):
                u, v = blocks(us[q]), blocks(wave[s, q])
                for k in range(2):
                    gr = gr + u[k] * v[k] + u[2 + k] * v[2 + k]
                    gi = gi + u[2 + k] * v[k] - u[k] * v[2 + k]
            gout[s, 0] = gr.astype(bf)
            gout[s, 1] = gi.astype(bf)

            @pl.when(y != s)
            def _():
                grad_copy(s, mine).start()

            @pl.when(y == s)
            def _():
                gin[mine] = gout[s]

            sr, si = screen(s)
            for q in range(pairs):
                wave[depth, q] = mul_columns(us[q], sr, -si)

        leave(depth - 1, us)

        def backward(k, carry):
            s = depth - 2 - k
            xs = [wave[depth, q] for q in range(pairs)]
            leave(s, propagate(tab, xs, prop[0] * UNIT_B**4, prop[1] * -(UNIT_B**4), BMODE))
            return carry

        lax.fori_loop(0, depth - 1, backward, 0)

    for p in range(slots):
        @pl.when(y != 2 * p + core)
        def _():
            grad_copy(0, p).wait_recv()

        got = dot(jnp.concatenate([gin[p, 0], gin[p, 1]], 0), cols_back[p]).astype(bf)
        for cb in range(4):
            for ri in range(2):
                gcols[cb, p * N : (p + 1) * N, ri * N : (ri + 1) * N] = got[ri * N : (ri + 1) * N, cb * N : (cb + 1) * N]

    def fold_rows(cb):
        return dot(rows_back[...], gcols[cb])

    def fold_left(k):
        lo, hi = pieces[k]
        return pltpu.make_async_remote_copy(
            src_ref=hout.at[0, :, lo:hi], dst_ref=hin.at[0, :, lo:hi],
            send_sem=fh_send.at[0, k], recv_sem=fh_recv.at[0, k], device_id=(y, t - 1), device_id_type=MESH)

    def fold_right(k):
        lo, hi = pieces[k]
        return pltpu.make_async_remote_copy(
            src_ref=hout.at[1, :, lo:hi], dst_ref=hin.at[1, :, lo:hi],
            send_sem=fh_send.at[1, k], recv_sem=fh_recv.at[1, k], device_id=(y, t + 1), device_id_type=MESH)

    for cb, way in ((0, 0), (3, 1)):
        got = fold_rows(cb).astype(bf)
        hout[way, 0] = got[:, :N]
        hout[way, 1] = got[:, N:]
    for k in range(3):
        @pl.when(has_left)
        def _():
            fold_left(k).start()

        @pl.when(has_right)
        def _():
            fold_right(k).start()

    for cb in (1, 2):
        got = fold_rows(cb)
        gframe[0, cb - 1] = got[:, :N]
        gframe[1, cb - 1] = got[:, N:]

    def fold_up():
        return pltpu.make_async_remote_copy(
            src_ref=vout.at[0], dst_ref=vin.at[0],
            send_sem=fv_send.at[0], recv_sem=fv_recv.at[0], device_id=(y, t - TCOLS), device_id_type=MESH)

    def fold_down():
        return pltpu.make_async_remote_copy(
            src_ref=vout.at[1], dst_ref=vin.at[1],
            send_sem=fv_send.at[1], recv_sem=fv_recv.at[1], device_id=(y, t + TCOLS), device_id_type=MESH)

    def take_sides(k):
        lo, hi = pieces[k]

        @pl.when(has_right)
        def _():
            fold_left(k).wait_recv()
            for ri in range(2):
                gframe[ri, 1, lo:hi] = gframe[ri, 1, lo:hi] + hin[0, ri, lo:hi].astype(f32)

        @pl.when(has_left)
        def _():
            fold_right(k).wait_recv()
            for ri in range(2):
                gframe[ri, 0, lo:hi] = gframe[ri, 0, lo:hi] + hin[1, ri, lo:hi].astype(f32)

    take_sides(0)
    vout[0] = gframe[:, :, 0:N].astype(bf)

    @pl.when(has_up)
    def _():
        fold_up().start()

    take_sides(1)
    vout[1] = gframe[:, :, 3 * N : 4 * N].astype(bf)

    @pl.when(has_down)
    def _():
        fold_down().start()

    take_sides(2)
    for ri in range(2):
        for cb in range(2):
            out[ri, :, cb * N : (cb + 1) * N] = gframe[ri, cb, N : 3 * N]

    @pl.when(has_up)
    def _():
        fold_down().wait_recv()
        for ri in range(2):
            for cb in range(2):
                at = (ri, slice(0, N), slice(cb * N, (cb + 1) * N))
                out[at] = out[at] + vin[1, ri, cb].astype(f32)

    @pl.when(has_down)
    def _():
        fold_up().wait_recv()
        for ri in range(2):
            for cb in range(2):
                at = (ri, slice(N, 2 * N), slice(cb * N, (cb + 1) * N))
                out[at] = out[at] + vin[0, ri, cb].astype(f32)

    @pl.when(has_down)
    def _():
        halo_down().wait_send()
        fold_down().wait_send()

    @pl.when(has_up)
    def _():
        halo_up().wait_send()
        fold_up().wait_send()

    @pl.when(has_right)
    def _():
        for k in range(3):
            halo_right(k).wait_send()
            fold_right(k).wait_send()

    @pl.when(has_left)
    def _():
        for k in range(3):
            halo_left(k).wait_send()
            fold_left(k).wait_send()

    for p in range(slots):
        @pl.when(y != 2 * p + core)
        def _():
            patch_copy(p, 0).wait_send()

    for s in range(depth):
        @pl.when(jnp.logical_and(lax.rem(y, 2) == core, y != s))
        def _():
            grad_copy(s, 0).wait_send()


def body(depth, tiles, transmission, probe_modes, propagator_phase, measured, counts, offsets):
    slots = offsets.shape[1]
    pairs = probe_modes.shape[0] // 2
    bf, f32 = jnp.bfloat16, jnp.float32
    vmem = pl.BlockSpec(memory_space=pltpu.VMEM)
    smem = pl.BlockSpec(memory_space=pltpu.SMEM)
    dma = pltpu.SemaphoreType.DMA
    grad = pl.pallas_call(
        functools.partial(kernel, depth, tiles, slots, pairs),
        out_shape=jax.ShapeDtypeStruct((2, 2 * N, 2 * N), f32),
        in_specs=[vmem, vmem, vmem, vmem, smem, smem, vmem],
        out_specs=vmem,
        scratch_shapes=[
            pltpu.VMEM((2, 4, 4 * N, N), bf),
            pltpu.VMEM((slots * N, 4 * N), bf),
            pltpu.VMEM((slots, 4 * N, N), bf),
            pltpu.VMEM((4 * N, slots * N), bf),
            pltpu.VMEM((slots, N, 4 * N), bf),
            pltpu.VMEM((slots, 2 * N, 4 * N), bf),
            pltpu.VMEM((slots, 2, N, N), bf),
            pltpu.VMEM((depth, 2, N, N), bf),
            pltpu.VMEM((depth + 1, pairs, 2 * N, 2 * N), f32),
            pltpu.VMEM((2, N, N), f32),
            pltpu.VMEM((depth, 2, N, N), bf),
            pltpu.VMEM((slots, 2, N, N), bf),
            pltpu.VMEM((4, slots * N, 2 * N), bf),
            pltpu.VMEM((2, 2, 4 * N, N), f32),
            pltpu.VMEM((2, 2, 4 * N, N), bf),
            pltpu.VMEM((2, 2, 4 * N, N), bf),
            pltpu.VMEM((2, 2, 2, N, N), bf),
            pltpu.VMEM((2, 2, 2, N, N), bf),
            dma((2,)), dma((2,)), dma((2, 3)), dma((2, 3)),
            dma((slots,)), dma((depth,)), dma((depth,)), dma((slots,)),
            dma((2, 3)), dma((2, 3)), dma((2,)), dma((2,)),
        ],
        compiler_params=pltpu.CompilerParams(
            collective_id=0, has_side_effects=True, vmem_limit_bytes=48 * 2**20
        ),
        cost_estimate=pl.CostEstimate(flops=2 * 10**10, bytes_accessed=3 * 2**20, transcendentals=2 * N * N),
    )(
        transmission[0, 0], probe_modes, propagator_phase, measured[0], counts, offsets.reshape(-1),
        jnp.asarray(TABLES),
    )
    return grad[None, None]


def solution(mesh):
    return jax.shard_map(
        functools.partial(body, mesh.shape["depth"], mesh.shape["tile"]),
        mesh=mesh,
        in_specs=(
            P("depth", "tile", None, None, None),
            P(),
            P(),
            P("tile", None, None, None),
            P("tile"),
            P("tile", None, None),
        ),
        out_specs=P("depth", "tile", None, None, None),
        check_vma=False,
    )
```

```python
import functools
import math

import jax
import jax.numpy as jnp
import ml_dtypes
import numpy as np
from jax import lax
from jax.experimental import pallas as pl
from jax.experimental.pallas import tpu as pltpu
from jax.sharding import PartitionSpec as P

TCOLS = 4
N = 128
MESH = pl.DeviceIdType.MESH
CLASS_SCALES = 1.2742026, 1.2925407, 1.5548331, 1.5449858, 1.3945649, 1.3043629, 1.3043644, 1.3043595


def dft_tables():
    k = np.arange(N)
    scale = np.array([CLASS_SCALES[-1 if j == 0 else (j & -j).bit_length() - 1] for j in range(N)])
    angle = -2 * np.pi * ((k[:, None] * k[None, :]) % N) / N
    exact = np.exp(1j * angle)
    held = exact * scale[:, None] * scale[None, :]
    re, im = held.real.astype(np.float32).astype(ml_dtypes.bfloat16), held.imag.astype(np.float32).astype(ml_dtypes.bfloat16)
    rounded = (re.astype(np.float64) + 1j * im.astype(np.float64)) / (scale[:, None] * scale[None, :])
    gain = (rounded * exact.conj()).sum(1).real / N
    g = np.block([[re, -im], [im, re]])
    after = 1 / (scale * gain * math.sqrt(N))
    before = 1 / scale
    outer = [np.outer(v, v) for v in (after * before, after, before, 1 / after)]
    return np.stack([g, g.T]), np.stack(outer).astype(np.float32)


TABLES, FACTORS = dft_tables()


def blocks(y):
    return y[:N, :N], y[:N, N:], y[N:, :N], y[N:, N:]


def square(a, b, c, d):
    return jnp.concatenate([jnp.concatenate([a, b], 1), jnp.concatenate([c, d], 1)], 0)


def swap(y):
    a, b, c, d = blocks(y)
    return square(a, c, b, d)


def dot(a, b):
    return jnp.dot(a, b, preferred_element_type=jnp.float32)


def left(tab, which, x):
    return dot(tab[which], x.astype(jnp.bfloat16))


def right(tab, which, x):
    return dot(x.astype(jnp.bfloat16), tab[which])


def mul_columns(x, sr, si):
    r1, r2, i1, i2 = blocks(x)
    return square(sr * r1 - si * i1, sr * r2 - si * i2, sr * i1 + si * r1, sr * i2 + si * r2)


def mul_rows(x, sr, si):
    r1, i1, r2, i2 = blocks(x)
    return square(sr * r1 - si * i1, sr * i1 + si * r1, sr * r2 - si * i2, sr * i2 + si * r2)


def propagate(tab, xs, hr, hi):
    xs = [swap(left(tab, 0, x)) for x in xs]
    xs = [mul_rows(right(tab, 1, x), hr, hi) for x in xs]
    xs = [swap(right(tab, 0, x)) for x in xs]
    return [left(tab, 1, x) for x in xs]


def kernel(
    depth, tiles, slots, pairs,
    own_hbm, probe_hbm, phase_hbm, measured_hbm, counts, offsets, tab_hbm, fac_hbm,
    out,
    own, probe, phase, measured, tab, fac,
    frame, rows_of, cols_of, rows_back, cols_back, cropped, patch, screens, wave, prop, gout, gin, gcols, gframe,
    hout, hin, vout, vin,
    own_sem, in_sem,
    v_send, v_recv, h_send, h_recv, p_send, p_recv, g_send, g_recv, fh_send, fh_recv, fv_send, fv_recv,
):
    y = lax.axis_index("depth")
    t = lax.axis_index("tile")
    core = lax.rem(t, 2)
    col = lax.rem(t, TCOLS)
    row = lax.div(t, TCOLS)
    has_up, has_down = row > 0, row < tiles // TCOLS - 1
    has_left, has_right = col > 0, col < TCOLS - 1
    bf = jnp.bfloat16
    f32 = jnp.float32

    def load_own(ri, half):
        part = (ri, slice(half * N, (half + 1) * N))
        return pltpu.make_async_copy(own_hbm.at[part], own.at[part], own_sem.at[ri, half])

    def load(k):
        src, dst = ((phase_hbm, phase), (probe_hbm, probe), (tab_hbm, tab), (measured_hbm, measured), (fac_hbm, fac))[k]
        return pltpu.make_async_copy(src, dst, in_sem.at[k])

    for ri in range(2):
        for half in range(2):
            load_own(ri, half).start()

    barrier = pltpu.get_barrier_semaphore()
    around = ((has_up, -TCOLS), (has_down, TCOLS), (has_left, -1), (has_right, 1))
    for there, by in around:
        @pl.when(there)
        def _():
            pl.semaphore_signal(barrier, inc=1, device_id=(y, t + by), device_id_type=MESH)
    for k in range(1, depth):
        pl.semaphore_signal(barrier, inc=1, device_id=(lax.rem(y + k, depth), t), device_id_type=MESH)

    for k in range(5):
        load(k).start()

    def outside(ri, shape):
        return jnp.full(shape, -1.0 if ri == 0 else 0.0, bf)


    @pl.when(jnp.logical_not(has_up))
    def _():
        for ri in range(2):
            frame[ri, 1:3, 0:N] = outside(ri, (2, N, N))

    @pl.when(jnp.logical_not(has_down))
    def _():
        for ri in range(2):
            frame[ri, 1:3, 3 * N : 4 * N] = outside(ri, (2, N, N))

    @pl.when(jnp.logical_not(has_left))
    def _():
        for ri in range(2):
            frame[ri, 0] = outside(ri, (4 * N, N))

    @pl.when(jnp.logical_not(has_right))
    def _():
        for ri in range(2):
            frame[ri, 3] = outside(ri, (4 * N, N))

    for ri in range(2):
        for half in range(2):
            load_own(ri, half).wait()
            for cb in range(2):
                got = own[ri, half * N : (half + 1) * N, cb * N : (cb + 1) * N]
                frame[ri, 1 + cb, (1 + half) * N : (2 + half) * N] = (got - 1.0 if ri == 0 else got).astype(bf)

    pl.semaphore_wait(
        barrier,
        depth - 1 + sum(there.astype(jnp.int32) for there, _ in around),
    )

    def halo_down(ri):
        return pltpu.make_async_remote_copy(
            src_ref=frame.at[ri, 1:3, 2 * N : 3 * N], dst_ref=frame.at[ri, 1:3, 0:N],
            send_sem=v_send.at[0, ri], recv_sem=v_recv.at[0, ri], device_id=(y, t + TCOLS), device_id_type=MESH)

    def halo_up(ri):
        return pltpu.make_async_remote_copy(
            src_ref=frame.at[ri, 1:3, N : 2 * N], dst_ref=frame.at[ri, 1:3, 3 * N : 4 * N],
            send_sem=v_send.at[1, ri], recv_sem=v_recv.at[1, ri], device_id=(y, t - TCOLS), device_id_type=MESH)

    pieces = ((0, N), (3 * N, 4 * N), (N, 3 * N))

    def halo_right(ri, k):
        lo, hi = pieces[k]
        return pltpu.make_async_remote_copy(
            src_ref=frame.at[ri, 2, lo:hi], dst_ref=frame.at[ri, 0, lo:hi],
            send_sem=h_send.at[0, ri, k], recv_sem=h_recv.at[0, ri, k], device_id=(y, t + 1), device_id_type=MESH)

    def halo_left(ri, k):
        lo, hi = pieces[k]
        return pltpu.make_async_remote_copy(
            src_ref=frame.at[ri, 1, lo:hi], dst_ref=frame.at[ri, 3, lo:hi],
            send_sem=h_send.at[1, ri, k], recv_sem=h_recv.at[1, ri, k], device_id=(y, t - 1), device_id_type=MESH)

    def sideways(ri, k):
        @pl.when(has_right)
        def _():
            halo_right(ri, k).start()

        @pl.when(has_left)
        def _():
            halo_left(ri, k).start()

    for ri in range(2):
        @pl.when(has_down)
        def _():
            halo_down(ri).start()

        @pl.when(has_up)
        def _():
            halo_up(ri).start()

    for ri in range(2):
        sideways(ri, 2)

    for p in range(slots):
        r, c = offsets[0, p], offsets[1, p]
        wide = lax.broadcasted_iota(jnp.int32, (N, 4 * N), 1) - lax.broadcasted_iota(jnp.int32, (N, 4 * N), 0)
        tall = lax.broadcasted_iota(jnp.int32, (4 * N, N), 0) - lax.broadcasted_iota(jnp.int32, (4 * N, N), 1)
        rows_of[p * N : (p + 1) * N] = jnp.where(wide == r, 1.0, 0.0).astype(bf)
        cols_back[p] = jnp.where(wide == c, 1.0, 0.0).astype(bf)
        rows_back[:, p * N : (p + 1) * N] = jnp.where(tall == r, 1.0, 0.0).astype(bf)
        cols_of[p] = jnp.where(tall == c, 1.0, 0.0).astype(bf)
    load(0).wait()
    angle = phase[...]
    hr, hi = jnp.cos(angle), jnp.sin(angle)
    load(4).wait()
    prop[0] = hr * fac[0]
    prop[1] = hi * fac[0]
    prop[2] = hr * fac[1]
    prop[3] = hi * fac[1]
    prop[4] = hr * fac[2]
    prop[5] = hi * fac[2]
    load(1).wait()
    for q in range(pairs):
        one, two = probe[2 * q], probe[2 * q + 1]
        wave[0, q] = square(one[0] * fac[3], two[0] * fac[3], one[1] * fac[3], two[1] * fac[3])
    load(2).wait()
    load(3).wait()

    def crop_rows(ri, one, other):
        got = dot(rows_of[...], jnp.concatenate([frame[ri, one], frame[ri, other]], 1)).astype(bf)
        for p in range(slots):
            cropped[ri, p, :, one * N : (one + 1) * N] = got[p * N : (p + 1) * N, :N]
            cropped[ri, p, :, other * N : (other + 1) * N] = got[p * N : (p + 1) * N, N:]

    def patch_copy(p, s, ri):
        return pltpu.make_async_remote_copy(
            src_ref=patch.at[p, ri], dst_ref=screens.at[s, ri],
            send_sem=p_send.at[p, ri], recv_sem=p_recv.at[s, ri], device_id=(2 * p + core, t), device_id_type=MESH)

    for ri in range(2):
        @pl.when(has_up)
        def _():
            halo_down(ri).wait_recv()

        sideways(ri, 0)

        @pl.when(has_down)
        def _():
            halo_up(ri).wait_recv()

        sideways(ri, 1)

    for ri in range(2):
        crop_rows(ri, 1, 2)

    for ri in range(2):
        for k in (2, 0, 1):
            @pl.when(has_left)
            def _():
                halo_right(ri, k).wait_recv()

            @pl.when(has_right)
            def _():
                halo_left(ri, k).wait_recv()

        crop_rows(ri, 0, 3)
        for p in range(slots):
            patch[p, ri] = dot(cropped[ri, p], cols_of[p]).astype(bf)

            @pl.when(y != 2 * p + core)
            def _():
                patch_copy(p, y, ri).start()

            @pl.when(y == 2 * p + core)
            def _():
                screens[y, ri] = patch[p, ri]

    mine = lax.div(y, 2)

    def grad_copy(s, p):
        return pltpu.make_async_remote_copy(
            src_ref=gout.at[s], dst_ref=gin.at[p],
            send_sem=g_send.at[s], recv_sem=g_recv.at[p], device_id=(s, t), device_id_type=MESH)

    @pl.when(lax.rem(y, 2) == core)
    def _():
        def screen(s):
            return (screens[s, 0].astype(f32) + 1.0) * fac[0], screens[s, 1].astype(f32) * fac[0]

        def arrive(s):
            @pl.when(y != s)
            def _():
                for ri in range(2):
                    patch_copy(0, s, ri).wait_recv()

        def forward(s, carry):
            arrive(s)
            sr, si = screen(s)
            xs = [mul_columns(wave[s, q], sr, si) for q in range(pairs)]
            xs = propagate(tab, xs, prop[0], prop[1])
            for q in range(pairs):
                wave[s + 1, q] = xs[q]
            return carry

        lax.fori_loop(0, depth - 1, forward, 0)
        arrive(depth - 1)
        sr, si = screen(depth - 1)
        xs = [mul_columns(wave[depth - 1, q], sr, si) for q in range(pairs)]
        xs = [swap(left(tab, 0, x)) for x in xs]
        xs = [mul_rows(right(tab, 1, x), prop[2], prop[3]) for x in xs]
        intensity = jnp.zeros((N, N), f32)
        for x in xs:
            for part in blocks(x):
                intensity = intensity + part * part
        valid = jnp.where(mine < counts[0], 4.0, 0.0)
        weight = (intensity - measured[mine]) * valid
        xs = [mul_rows(x, prop[4] * weight, -prop[5] * weight) for x in xs]
        xs = [swap(right(tab, 0, x)) for x in xs]
        us = [left(tab, 1, x) for x in xs]

        def leave(s, us):
            gr = jnp.zeros((N, N), f32)
            gi = jnp.zeros((N, N), f32)
            for q in range(pairs):
                u, v = blocks(us[q]), blocks(wave[s, q])
                for k in range(2):
                    gr = gr + u[k] * v[k] + u[2 + k] * v[2 + k]
                    gi = gi + u[2 + k] * v[k] - u[k] * v[2 + k]
            back = fac[1] * fac[1]
            gout[s, 0] = (gr * back).astype(bf)
            gout[s, 1] = (gi * back).astype(bf)

            @pl.when(y != s)
            def _():
                grad_copy(s, mine).start()

            @pl.when(y == s)
            def _():
                gin[mine] = gout[s]

            sr, si = screen(s)
            for q in range(pairs):
                wave[depth, q] = mul_columns(us[q], sr, -si)

        leave(depth - 1, us)

        def backward(k, carry):
            s = depth - 2 - k
            xs = [wave[depth, q] for q in range(pairs)]
            leave(s, propagate(tab, xs, prop[0], -prop[1]))
            return carry

        lax.fori_loop(0, depth - 1, backward, 0)

    for p in range(slots):
        @pl.when(y != 2 * p + core)
        def _():
            grad_copy(0, p).wait_recv()

        got = dot(jnp.concatenate([gin[p, 0], gin[p, 1]], 0), cols_back[p]).astype(bf)
        for ri in range(2):
            for cb in range(4):
                at = (0, 2, 3, 1)[cb]
                gcols[ri, p * N : (p + 1) * N, at * N : (at + 1) * N] = got[ri * N : (ri + 1) * N, cb * N : (cb + 1) * N]

    def fold_left(ri, k):
        lo, hi = pieces[k]
        return pltpu.make_async_remote_copy(
            src_ref=hout.at[0, ri, lo:hi], dst_ref=hin.at[0, ri, lo:hi],
            send_sem=fh_send.at[0, ri, k], recv_sem=fh_recv.at[0, ri, k], device_id=(y, t - 1), device_id_type=MESH)

    def fold_right(ri, k):
        lo, hi = pieces[k]
        return pltpu.make_async_remote_copy(
            src_ref=hout.at[1, ri, lo:hi], dst_ref=hin.at[1, ri, lo:hi],
            send_sem=fh_send.at[1, ri, k], recv_sem=fh_recv.at[1, ri, k], device_id=(y, t + 1), device_id_type=MESH)

    def send_sides(ri, k):
        @pl.when(has_left)
        def _():
            fold_left(ri, k).start()

        @pl.when(has_right)
        def _():
            fold_right(ri, k).start()

    for ri in range(2):
        got = dot(rows_back[...], gcols[ri, :, : 2 * N]).astype(bf)
        hout[0, ri] = got[:, :N]
        hout[1, ri] = got[:, N:]
        send_sides(ri, 0)
        send_sides(ri, 1)
    for ri in range(2):
        send_sides(ri, 2)
    for ri in range(2):
        got = dot(rows_back[...], gcols[ri, :, 2 * N :])
        gframe[ri, 0] = got[:, :N]
        gframe[ri, 1] = got[:, N:]

    def fold_up(ri):
        return pltpu.make_async_remote_copy(
            src_ref=vout.at[0, ri], dst_ref=vin.at[0, ri],
            send_sem=fv_send.at[0, ri], recv_sem=fv_recv.at[0, ri], device_id=(y, t - TCOLS), device_id_type=MESH)

    def fold_down(ri):
        return pltpu.make_async_remote_copy(
            src_ref=vout.at[1, ri], dst_ref=vin.at[1, ri],
            send_sem=fv_send.at[1, ri], recv_sem=fv_recv.at[1, ri], device_id=(y, t + TCOLS), device_id_type=MESH)

    def take_sides(ri, k):
        lo, hi = pieces[k]

        @pl.when(has_right)
        def _():
            fold_left(ri, k).wait_recv()
            gframe[ri, 1, lo:hi] = gframe[ri, 1, lo:hi] + hin[0, ri, lo:hi].astype(f32)

        @pl.when(has_left)
        def _():
            fold_right(ri, k).wait_recv()
            gframe[ri, 0, lo:hi] = gframe[ri, 0, lo:hi] + hin[1, ri, lo:hi].astype(f32)

    for ri in range(2):
        take_sides(ri, 0)
        vout[0, ri] = gframe[ri, :, 0:N].astype(bf)

        @pl.when(has_up)
        def _():
            fold_up(ri).start()

        take_sides(ri, 1)
        vout[1, ri] = gframe[ri, :, 3 * N : 4 * N].astype(bf)

        @pl.when(has_down)
        def _():
            fold_down(ri).start()

    for ri in range(2):
        take_sides(ri, 2)
        for cb in range(2):
            out[ri, :, cb * N : (cb + 1) * N] = gframe[ri, cb, N : 3 * N]

    for ri in range(2):
        @pl.when(has_up)
        def _():
            fold_down(ri).wait_recv()
            for cb in range(2):
                at = (ri, slice(0, N), slice(cb * N, (cb + 1) * N))
                out[at] = out[at] + vin[1, ri, cb].astype(f32)

        @pl.when(has_down)
        def _():
            fold_up(ri).wait_recv()
            for cb in range(2):
                at = (ri, slice(N, 2 * N), slice(cb * N, (cb + 1) * N))
                out[at] = out[at] + vin[0, ri, cb].astype(f32)

    for ri in range(2):
        @pl.when(has_down)
        def _():
            halo_down(ri).wait_send()
            fold_down(ri).wait_send()

        @pl.when(has_up)
        def _():
            halo_up(ri).wait_send()
            fold_up(ri).wait_send()

        @pl.when(has_right)
        def _():
            for k in range(3):
                halo_right(ri, k).wait_send()
                fold_right(ri, k).wait_send()

        @pl.when(has_left)
        def _():
            for k in range(3):
                halo_left(ri, k).wait_send()
                fold_left(ri, k).wait_send()

        for p in range(slots):
            @pl.when(y != 2 * p + core)
            def _():
                patch_copy(p, 0, ri).wait_send()

    for s in range(depth):
        @pl.when(jnp.logical_and(lax.rem(y, 2) == core, y != s))
        def _():
            grad_copy(s, 0).wait_send()


def body(depth, tiles, transmission, probe_modes, propagator_phase, measured, counts, offsets):
    slots = offsets.shape[1]
    pairs = probe_modes.shape[0] // 2
    bf, f32 = jnp.bfloat16, jnp.float32
    vmem = pl.BlockSpec(memory_space=pltpu.VMEM)
    hbm = pl.BlockSpec(memory_space=pl.ANY)
    smem = pl.BlockSpec(memory_space=pltpu.SMEM)
    dma = pltpu.SemaphoreType.DMA
    grad = pl.pallas_call(
        functools.partial(kernel, depth, tiles, slots, pairs),
        out_shape=jax.ShapeDtypeStruct((2, 2 * N, 2 * N), f32),
        in_specs=[hbm, hbm, hbm, hbm, smem, smem, hbm, hbm],
        out_specs=vmem,
        scratch_shapes=[
            pltpu.VMEM((2, 2 * N, 2 * N), f32),
            pltpu.VMEM(probe_modes.shape, f32),
            pltpu.VMEM((N, N), f32),
            pltpu.VMEM((slots, N, N), f32),
            pltpu.VMEM(TABLES.shape, bf),
            pltpu.VMEM(FACTORS.shape, f32),
            pltpu.VMEM((2, 4, 4 * N, N), bf),
            pltpu.VMEM((slots * N, 4 * N), bf),
            pltpu.VMEM((slots, 4 * N, N), bf),
            pltpu.VMEM((4 * N, slots * N), bf),
            pltpu.VMEM((slots, N, 4 * N), bf),
            pltpu.VMEM((2, slots, N, 4 * N), bf),
            pltpu.VMEM((slots, 2, N, N), bf),
            pltpu.VMEM((depth, 2, N, N), bf),
            pltpu.VMEM((depth + 1, pairs, 2 * N, 2 * N), f32),
            pltpu.VMEM((6, N, N), f32),
            pltpu.VMEM((depth, 2, N, N), bf),
            pltpu.VMEM((slots, 2, N, N), bf),
            pltpu.VMEM((2, slots * N, 4 * N), bf),
            pltpu.VMEM((2, 2, 4 * N, N), f32),
            pltpu.VMEM((2, 2, 4 * N, N), bf),
            pltpu.VMEM((2, 2, 4 * N, N), bf),
            pltpu.VMEM((2, 2, 2, N, N), bf),
            pltpu.VMEM((2, 2, 2, N, N), bf),
            dma((2, 2)), dma((5,)),
            dma((2, 2)), dma((2, 2)), dma((2, 2, 3)), dma((2, 2, 3)),
            dma((slots, 2)), dma((depth, 2)), dma((depth,)), dma((slots,)),
            dma((2, 2, 3)), dma((2, 2, 3)), dma((2, 2)), dma((2, 2)),
        ],
        compiler_params=pltpu.CompilerParams(
            collective_id=0, has_side_effects=True, vmem_limit_bytes=56 * 2**20
        ),
        cost_estimate=pl.CostEstimate(flops=2 * 10**10, bytes_accessed=3 * 2**20, transcendentals=2 * N * N),
    )(
        transmission[0, 0], probe_modes, propagator_phase, measured[0], counts, jnp.transpose(offsets[0]),
        jnp.asarray(TABLES), jnp.asarray(FACTORS),
    )
    return grad[None, None]


def solution(mesh):
    return jax.shard_map(
        functools.partial(body, mesh.shape["depth"], mesh.shape["tile"]),
        mesh=mesh,
        in_specs=(
            P("depth", "tile", None, None, None),
            P(),
            P(),
            P("tile", None, None, None),
            P("tile"),
            P("tile", None, None),
        ),
        out_specs=P("depth", "tile", None, None, None),
        check_vma=False,
    )
```

```python
import functools
import math

import jax
import jax.numpy as jnp
import ml_dtypes
import numpy as np
from jax import lax
from jax.experimental import pallas as pl
from jax.experimental.pallas import tpu as pltpu
from jax.sharding import PartitionSpec as P

TCOLS = 4
N = 128
WORKERS = ((0, 1, 3, 6), (1, 2, 5, 7))
MESH = pl.DeviceIdType.MESH
CLASS_SCALES = 1.2742026, 1.2925407, 1.5548331, 1.5449858, 1.3945649, 1.3043629, 1.3043644, 1.3043595


def dft_tables():
    k = np.arange(N)
    scale = np.array([CLASS_SCALES[-1 if j == 0 else (j & -j).bit_length() - 1] for j in range(N)])
    angle = -2 * np.pi * ((k[:, None] * k[None, :]) % N) / N
    exact = np.exp(1j * angle)
    held = exact * scale[:, None] * scale[None, :]
    re, im = held.real.astype(np.float32).astype(ml_dtypes.bfloat16), held.imag.astype(np.float32).astype(ml_dtypes.bfloat16)
    rounded = (re.astype(np.float64) + 1j * im.astype(np.float64)) / (scale[:, None] * scale[None, :])
    gain = (rounded * exact.conj()).sum(1).real / N
    g = np.block([[re, -im], [im, re]])
    after = 1 / (scale * gain * math.sqrt(N))
    before = 1 / scale
    outer = [np.outer(v, v) for v in (after * before, after, before, 1 / after)]
    return np.stack([g, g.T]), np.stack(outer).astype(np.float32)


TABLES, FACTORS = dft_tables()


def blocks(y):
    return y[:N, :N], y[:N, N:], y[N:, :N], y[N:, N:]


def square(a, b, c, d):
    return jnp.concatenate([jnp.concatenate([a, b], 1), jnp.concatenate([c, d], 1)], 0)


def swap(y):
    a, b, c, d = blocks(y)
    return square(a, c, b, d)


def dot(a, b):
    return jnp.dot(a, b, preferred_element_type=jnp.float32)


def left(tab, which, x):
    x = x.astype(jnp.bfloat16)
    return jnp.concatenate([dot(tab[which, :N], x), dot(tab[which, N:], x)], 0)


def right(tab, which, x):
    x = x.astype(jnp.bfloat16)
    return jnp.concatenate([dot(x[:N], tab[which]), dot(x[N:], tab[which])], 0)


def mul_columns(x, sr, si):
    r1, r2, i1, i2 = blocks(x)
    return square(sr * r1 - si * i1, sr * r2 - si * i2, sr * i1 + si * r1, sr * i2 + si * r2)


def mul_rows(x, sr, si):
    r1, i1, r2, i2 = blocks(x)
    return square(sr * r1 - si * i1, sr * i1 + si * r1, sr * r2 - si * i2, sr * i2 + si * r2)


def propagate(tab, xs, hr, hi):
    xs = [swap(left(tab, 0, x)) for x in xs]
    xs = [mul_rows(right(tab, 1, x), hr, hi) for x in xs]
    xs = [swap(right(tab, 0, x)) for x in xs]
    return [left(tab, 1, x) for x in xs]


def kernel(
    depth, tiles, slots, pairs,
    own_hbm, probe_hbm, phase_hbm, measured_hbm, counts, offsets, tab_hbm, fac_hbm,
    out,
    own, probe, phase, measured, tab, fac,
    frame, rows_of, cols_of, rows_back, cols_back, cropped, patch, screens, wave, prop, gout, gin, gcols, gframe,
    hout, hin, vout, vin,
    own_sem, in_sem,
    v_send, v_recv, h_send, h_recv, p_send, p_recv, g_send, g_recv, fh_send, fh_recv, fv_send, fv_recv,
):
    y = lax.axis_index("depth")
    t = lax.axis_index("tile")
    core = lax.rem(t, 2)
    col = lax.rem(t, TCOLS)
    row = lax.div(t, TCOLS)
    has_up, has_down = row > 0, row < tiles // TCOLS - 1
    has_left, has_right = col > 0, col < TCOLS - 1
    bf = jnp.bfloat16
    f32 = jnp.float32

    def worker(p):
        return WORKERS[0][p] + core * (WORKERS[1][p] - WORKERS[0][p])

    def load_own(ri, half):
        part = (ri, slice(half * N, (half + 1) * N))
        return pltpu.make_async_copy(own_hbm.at[part], own.at[part], own_sem.at[ri, half])

    def load(k):
        src, dst = ((phase_hbm, phase), (probe_hbm, probe), (tab_hbm, tab), (measured_hbm, measured), (fac_hbm, fac))[k]
        return pltpu.make_async_copy(src, dst, in_sem.at[k])

    for ri in range(2):
        for half in range(2):
            load_own(ri, half).start()

    barrier = pltpu.get_barrier_semaphore()
    around = ((has_up, -TCOLS), (has_down, TCOLS), (has_left, -1), (has_right, 1))
    for there, by in around:
        @pl.when(there)
        def _():
            pl.semaphore_signal(barrier, inc=1, device_id=(y, t + by), device_id_type=MESH)
    for k in range(1, depth):
        pl.semaphore_signal(barrier, inc=1, device_id=(lax.rem(y + k, depth), t), device_id_type=MESH)

    for k in range(5):
        load(k).start()

    def outside(ri, shape):
        return jnp.full(shape, -1.0 if ri == 0 else 0.0, bf)


    @pl.when(jnp.logical_not(has_up))
    def _():
        for ri in range(2):
            frame[ri, 1:3, 0:N] = outside(ri, (2, N, N))

    @pl.when(jnp.logical_not(has_down))
    def _():
        for ri in range(2):
            frame[ri, 1:3, 3 * N : 4 * N] = outside(ri, (2, N, N))

    @pl.when(jnp.logical_not(has_left))
    def _():
        for ri in range(2):
            frame[ri, 0] = outside(ri, (4 * N, N))

    @pl.when(jnp.logical_not(has_right))
    def _():
        for ri in range(2):
            frame[ri, 3] = outside(ri, (4 * N, N))

    for ri in range(2):
        for half in range(2):
            load_own(ri, half).wait()
            for cb in range(2):
                got = own[ri, half * N : (half + 1) * N, cb * N : (cb + 1) * N]
                frame[ri, 1 + cb, (1 + half) * N : (2 + half) * N] = (got - 1.0 if ri == 0 else got).astype(bf)

    pl.semaphore_wait(
        barrier,
        depth - 1 + sum(there.astype(jnp.int32) for there, _ in around),
    )

    def halo_down(ri):
        return pltpu.make_async_remote_copy(
            src_ref=frame.at[ri, 1:3, 2 * N : 3 * N], dst_ref=frame.at[ri, 1:3, 0:N],
            send_sem=v_send.at[0, ri], recv_sem=v_recv.at[0, ri], device_id=(y, t + TCOLS), device_id_type=MESH)

    def halo_up(ri):
        return pltpu.make_async_remote_copy(
            src_ref=frame.at[ri, 1:3, N : 2 * N], dst_ref=frame.at[ri, 1:3, 3 * N : 4 * N],
            send_sem=v_send.at[1, ri], recv_sem=v_recv.at[1, ri], device_id=(y, t - TCOLS), device_id_type=MESH)

    pieces = ((0, N), (3 * N, 4 * N), (N, 3 * N))

    def halo_right(ri, k):
        lo, hi = pieces[k]
        return pltpu.make_async_remote_copy(
            src_ref=frame.at[ri, 2, lo:hi], dst_ref=frame.at[ri, 0, lo:hi],
            send_sem=h_send.at[0, ri, k], recv_sem=h_recv.at[0, ri, k], device_id=(y, t + 1), device_id_type=MESH)

    def halo_left(ri, k):
        lo, hi = pieces[k]
        return pltpu.make_async_remote_copy(
            src_ref=frame.at[ri, 1, lo:hi], dst_ref=frame.at[ri, 3, lo:hi],
            send_sem=h_send.at[1, ri, k], recv_sem=h_recv.at[1, ri, k], device_id=(y, t - 1), device_id_type=MESH)

    def sideways(ri, k):
        @pl.when(has_right)
        def _():
            halo_right(ri, k).start()

        @pl.when(has_left)
        def _():
            halo_left(ri, k).start()

    def send_halo(ri):
        @pl.when(has_down)
        def _():
            halo_down(ri).start()

        @pl.when(has_up)
        def _():
            halo_up(ri).start()

        sideways(ri, 2)

    send_halo(0)

    for p in range(slots):
        r, c = offsets[0, p], offsets[1, p]
        wide = lax.broadcasted_iota(jnp.int32, (N, 4 * N), 1) - lax.broadcasted_iota(jnp.int32, (N, 4 * N), 0)
        tall = lax.broadcasted_iota(jnp.int32, (4 * N, N), 0) - lax.broadcasted_iota(jnp.int32, (4 * N, N), 1)
        rows_of[p * N : (p + 1) * N] = jnp.where(wide == r, 1.0, 0.0).astype(bf)
        cols_back[p] = jnp.where(wide == c, 1.0, 0.0).astype(bf)
        rows_back[:, p * N : (p + 1) * N] = jnp.where(tall == r, 1.0, 0.0).astype(bf)
        cols_of[p] = jnp.where(tall == c, 1.0, 0.0).astype(bf)
    load(0).wait()
    angle = phase[...]
    hr, hi = jnp.cos(angle), jnp.sin(angle)
    load(4).wait()
    prop[0] = hr * fac[0]
    prop[1] = hi * fac[0]
    prop[2] = hr * fac[1]
    prop[3] = hi * fac[1]
    prop[4] = hr * fac[2]
    prop[5] = hi * fac[2]
    load(1).wait()
    for q in range(pairs):
        one, two = probe[2 * q], probe[2 * q + 1]
        wave[0, q] = square(one[0] * fac[3], two[0] * fac[3], one[1] * fac[3], two[1] * fac[3])
    load(2).wait()
    load(3).wait()

    def crop_rows(ri, one, other):
        got = dot(rows_of[...], jnp.concatenate([frame[ri, one], frame[ri, other]], 1)).astype(bf)
        for p in range(slots):
            cropped[ri, p, :, one * N : (one + 1) * N] = got[p * N : (p + 1) * N, :N]
            cropped[ri, p, :, other * N : (other + 1) * N] = got[p * N : (p + 1) * N, N:]

    def patch_copy(p, s, ri):
        return pltpu.make_async_remote_copy(
            src_ref=patch.at[p, ri], dst_ref=screens.at[s, ri],
            send_sem=p_send.at[p, ri], recv_sem=p_recv.at[s, ri], device_id=(worker(p), t), device_id_type=MESH)

    def take_rows(ri):
        @pl.when(has_up)
        def _():
            halo_down(ri).wait_recv()

        sideways(ri, 0)

        @pl.when(has_down)
        def _():
            halo_up(ri).wait_recv()

        sideways(ri, 1)

    take_rows(0)
    send_halo(1)
    for ri in range(2):
        if ri == 1:
            take_rows(1)
        crop_rows(ri, 1, 2)
        for k in (2, 0, 1):
            @pl.when(has_left)
            def _():
                halo_right(ri, k).wait_recv()

            @pl.when(has_right)
            def _():
                halo_left(ri, k).wait_recv()

        crop_rows(ri, 0, 3)
        for p in range(slots):
            patch[p, ri] = dot(cropped[ri, p], cols_of[p]).astype(bf)

        for p in range(slots):
            @pl.when(y != worker(p))
            def _():
                patch_copy(p, y, ri).start()

            @pl.when(y == worker(p))
            def _():
                screens[y, ri] = patch[p, ri]

    mine = sum(p * (y == worker(p)).astype(jnp.int32) for p in range(slots))
    working = sum((y == worker(p)).astype(jnp.int32) for p in range(slots)) > 0

    def grad_copy(s, p, ri):
        return pltpu.make_async_remote_copy(
            src_ref=gout.at[s, ri], dst_ref=gin.at[p, ri],
            send_sem=g_send.at[s, ri], recv_sem=g_recv.at[p, ri], device_id=(s, t), device_id_type=MESH)

    @pl.when(working)
    def _():
        def screen(s):
            return (screens[s, 0].astype(f32) + 1.0) * fac[0], screens[s, 1].astype(f32) * fac[0]

        def arrive(s):
            @pl.when(y != s)
            def _():
                for ri in range(2):
                    patch_copy(0, s, ri).wait_recv()

        def forward(s, carry):
            arrive(s)
            sr, si = screen(s)
            xs = [mul_columns(wave[s, q], sr, si) for q in range(pairs)]
            xs = propagate(tab, xs, prop[0], prop[1])
            for q in range(pairs):
                wave[s + 1, q] = xs[q]
            return carry

        lax.fori_loop(0, depth - 1, forward, 0)
        arrive(depth - 1)
        sr, si = screen(depth - 1)
        xs = [mul_columns(wave[depth - 1, q], sr, si) for q in range(pairs)]
        xs = [swap(left(tab, 0, x)) for x in xs]
        xs = [mul_rows(right(tab, 1, x), prop[2], prop[3]) for x in xs]
        intensity = jnp.zeros((N, N), f32)
        for x in xs:
            for part in blocks(x):
                intensity = intensity + part * part
        valid = jnp.where(mine < counts[0], 4.0, 0.0)
        weight = (intensity - measured[mine]) * valid
        xs = [mul_rows(x, prop[4] * weight, -prop[5] * weight) for x in xs]
        xs = [swap(right(tab, 0, x)) for x in xs]
        us = [left(tab, 1, x) for x in xs]

        for q in range(pairs):
            wave[depth, q] = us[q]

        def gradient(s, us):
            gr = jnp.zeros((N, N), f32)
            gi = jnp.zeros((N, N), f32)
            for q in range(pairs):
                u, v = blocks(us[q]), blocks(wave[s, q])
                for k in range(2):
                    gr = gr + u[k] * v[k] + u[2 + k] * v[2 + k]
                    gi = gi + u[2 + k] * v[k] - u[k] * v[2 + k]
            back = fac[1] * fac[1]
            gout[s, 0] = (gr * back).astype(bf)
            gout[s, 1] = (gi * back).astype(bf)

        def leave(s):
            @pl.when(y != s)
            def _():
                for ri in range(2):
                    grad_copy(s, mine, ri).start()

            @pl.when(y == s)
            def _():
                gin[mine] = gout[s]

        def backward(k, carry):
            s = depth - 1 - k
            us = [wave[depth, q] for q in range(pairs)]
            sr, si = screen(s)
            xs = propagate(tab, [mul_columns(u, sr, -si) for u in us], prop[0], -prop[1])
            gradient(s, us)
            for q in range(pairs):
                wave[depth, q] = xs[q]
            leave(s)
            return carry

        lax.fori_loop(0, depth - 1, backward, 0)
        gradient(0, [wave[depth, q] for q in range(pairs)])
        leave(0)

    def fold_left(ri, k):
        lo, hi = pieces[k]
        return pltpu.make_async_remote_copy(
            src_ref=hout.at[0, ri, lo:hi], dst_ref=hin.at[0, ri, lo:hi],
            send_sem=fh_send.at[0, ri, k], recv_sem=fh_recv.at[0, ri, k], device_id=(y, t - 1), device_id_type=MESH)

    def fold_right(ri, k):
        lo, hi = pieces[k]
        return pltpu.make_async_remote_copy(
            src_ref=hout.at[1, ri, lo:hi], dst_ref=hin.at[1, ri, lo:hi],
            send_sem=fh_send.at[1, ri, k], recv_sem=fh_recv.at[1, ri, k], device_id=(y, t + 1), device_id_type=MESH)

    def send_sides(ri, k):
        @pl.when(has_left)
        def _():
            fold_left(ri, k).start()

        @pl.when(has_right)
        def _():
            fold_right(ri, k).start()

    for ri in range(2):
        for p in range(slots):
            @pl.when(y != worker(p))
            def _():
                grad_copy(0, p, ri).wait_recv()

        for p in range(slots):
            got = dot(gin[p, ri], cols_back[p]).astype(bf)
            for cb in range(4):
                at = (0, 2, 3, 1)[cb]
                gcols[ri, p * N : (p + 1) * N, at * N : (at + 1) * N] = got[:, cb * N : (cb + 1) * N]
        got = dot(rows_back[...], gcols[ri, :, : 2 * N]).astype(bf)
        hout[0, ri] = got[:, :N]
        hout[1, ri] = got[:, N:]
        send_sides(ri, 0)
        send_sides(ri, 1)
        got = dot(rows_back[...], gcols[ri, :, 2 * N :])
        gframe[ri, 0] = got[:, :N]
        gframe[ri, 1] = got[:, N:]

    def fold_up(ri):
        return pltpu.make_async_remote_copy(
            src_ref=vout.at[0, ri], dst_ref=vin.at[0, ri],
            send_sem=fv_send.at[0, ri], recv_sem=fv_recv.at[0, ri], device_id=(y, t - TCOLS), device_id_type=MESH)

    def fold_down(ri):
        return pltpu.make_async_remote_copy(
            src_ref=vout.at[1, ri], dst_ref=vin.at[1, ri],
            send_sem=fv_send.at[1, ri], recv_sem=fv_recv.at[1, ri], device_id=(y, t + TCOLS), device_id_type=MESH)

    def take_sides(ri, k):
        lo, hi = pieces[k]

        @pl.when(has_right)
        def _():
            fold_left(ri, k).wait_recv()
            gframe[ri, 1, lo:hi] = gframe[ri, 1, lo:hi] + hin[0, ri, lo:hi].astype(f32)

        @pl.when(has_left)
        def _():
            fold_right(ri, k).wait_recv()
            gframe[ri, 0, lo:hi] = gframe[ri, 0, lo:hi] + hin[1, ri, lo:hi].astype(f32)

    for ri in range(2):
        take_sides(ri, 0)
        vout[0, ri] = gframe[ri, :, 0:N].astype(bf)

        @pl.when(has_up)
        def _():
            fold_up(ri).start()

        take_sides(ri, 1)
        vout[1, ri] = gframe[ri, :, 3 * N : 4 * N].astype(bf)

        @pl.when(has_down)
        def _():
            fold_down(ri).start()

        send_sides(ri, 2)

    for ri in range(2):
        take_sides(ri, 2)
        for cb in range(2):
            out[ri, :, cb * N : (cb + 1) * N] = gframe[ri, cb, N : 3 * N]

    for ri in range(2):
        @pl.when(has_up)
        def _():
            fold_down(ri).wait_recv()
            for cb in range(2):
                at = (ri, slice(0, N), slice(cb * N, (cb + 1) * N))
                out[at] = out[at] + vin[1, ri, cb].astype(f32)

        @pl.when(has_down)
        def _():
            fold_up(ri).wait_recv()
            for cb in range(2):
                at = (ri, slice(N, 2 * N), slice(cb * N, (cb + 1) * N))
                out[at] = out[at] + vin[0, ri, cb].astype(f32)

    for ri in range(2):
        @pl.when(has_down)
        def _():
            halo_down(ri).wait_send()
            fold_down(ri).wait_send()

        @pl.when(has_up)
        def _():
            halo_up(ri).wait_send()
            fold_up(ri).wait_send()

        @pl.when(has_right)
        def _():
            for k in range(3):
                halo_right(ri, k).wait_send()
                fold_right(ri, k).wait_send()

        @pl.when(has_left)
        def _():
            for k in range(3):
                halo_left(ri, k).wait_send()
                fold_left(ri, k).wait_send()

        for p in range(slots):
            @pl.when(y != worker(p))
            def _():
                patch_copy(p, 0, ri).wait_send()

    for s in range(depth):
        @pl.when(jnp.logical_and(working, y != s))
        def _():
            for ri in range(2):
                grad_copy(s, 0, ri).wait_send()


def body(depth, tiles, transmission, probe_modes, propagator_phase, measured, counts, offsets):
    slots = offsets.shape[1]
    pairs = probe_modes.shape[0] // 2
    bf, f32 = jnp.bfloat16, jnp.float32
    vmem = pl.BlockSpec(memory_space=pltpu.VMEM)
    hbm = pl.BlockSpec(memory_space=pl.ANY)
    smem = pl.BlockSpec(memory_space=pltpu.SMEM)
    dma = pltpu.SemaphoreType.DMA
    grad = pl.pallas_call(
        functools.partial(kernel, depth, tiles, slots, pairs),
        out_shape=pltpu.VMEM((2, 2 * N, 2 * N), f32),
        in_specs=[hbm, hbm, hbm, hbm, smem, smem, hbm, hbm],
        out_specs=vmem,
        scratch_shapes=[
            pltpu.VMEM((2, 2 * N, 2 * N), f32),
            pltpu.VMEM(probe_modes.shape, f32),
            pltpu.VMEM((N, N), f32),
            pltpu.VMEM((slots, N, N), f32),
            pltpu.VMEM(TABLES.shape, bf),
            pltpu.VMEM(FACTORS.shape, f32),
            pltpu.VMEM((2, 4, 4 * N, N), bf),
            pltpu.VMEM((slots * N, 4 * N), bf),
            pltpu.VMEM((slots, 4 * N, N), bf),
            pltpu.VMEM((4 * N, slots * N), bf),
            pltpu.VMEM((slots, N, 4 * N), bf),
            pltpu.VMEM((2, slots, N, 4 * N), bf),
            pltpu.VMEM((slots, 2, N, N), bf),
            pltpu.VMEM((depth, 2, N, N), bf),
            pltpu.VMEM((depth + 1, pairs, 2 * N, 2 * N), f32),
            pltpu.VMEM((6, N, N), f32),
            pltpu.VMEM((depth, 2, N, N), bf),
            pltpu.VMEM((slots, 2, N, N), bf),
            pltpu.VMEM((2, slots * N, 4 * N), bf),
            pltpu.VMEM((2, 2, 4 * N, N), f32),
            pltpu.VMEM((2, 2, 4 * N, N), bf),
            pltpu.VMEM((2, 2, 4 * N, N), bf),
            pltpu.VMEM((2, 2, 2, N, N), bf),
            pltpu.VMEM((2, 2, 2, N, N), bf),
            dma((2, 2)), dma((5,)),
            dma((2, 2)), dma((2, 2)), dma((2, 2, 3)), dma((2, 2, 3)),
            dma((slots, 2)), dma((depth, 2)), dma((depth, 2)), dma((slots, 2)),
            dma((2, 2, 3)), dma((2, 2, 3)), dma((2, 2)), dma((2, 2)),
        ],
        compiler_params=pltpu.CompilerParams(
            collective_id=0, has_side_effects=True, vmem_limit_bytes=56 * 2**20
        ),
        cost_estimate=pl.CostEstimate(flops=2 * 10**10, bytes_accessed=3 * 2**20, transcendentals=2 * N * N),
    )(
        transmission[0, 0], probe_modes, propagator_phase, measured[0], counts, jnp.transpose(offsets[0]),
        jnp.asarray(TABLES), jnp.asarray(FACTORS),
    )
    return grad[None, None]


def solution(mesh):
    return jax.shard_map(
        functools.partial(body, mesh.shape["depth"], mesh.shape["tile"]),
        mesh=mesh,
        in_specs=(
            P("depth", "tile", None, None, None),
            P(),
            P(),
            P("tile", None, None, None),
            P("tile"),
            P("tile", None, None),
        ),
        out_specs=P("depth", "tile", None, None, None),
        check_vma=False,
    )
```

```python
import functools
import math

import jax
import jax.numpy as jnp
import ml_dtypes
import numpy as np
from jax import lax
from jax.experimental import pallas as pl
from jax.experimental.pallas import tpu as pltpu
from jax.sharding import PartitionSpec as P

TCOLS = 4
N = 128
WORKERS = ((0, 1, 3, 6), (1, 2, 5, 7))
MESH = pl.DeviceIdType.MESH
CLASS_SCALES = 1.2742026, 1.2925407, 1.5548331, 1.5449858, 1.3945649, 1.3043629, 1.3043644, 1.3043595


def dft_tables():
    k = np.arange(N)
    scale = np.array([CLASS_SCALES[-1 if j == 0 else (j & -j).bit_length() - 1] for j in range(N)])
    angle = -2 * np.pi * ((k[:, None] * k[None, :]) % N) / N
    exact = np.exp(1j * angle)
    held = exact * scale[:, None] * scale[None, :]
    re, im = held.real.astype(np.float32).astype(ml_dtypes.bfloat16), held.imag.astype(np.float32).astype(ml_dtypes.bfloat16)
    rounded = (re.astype(np.float64) + 1j * im.astype(np.float64)) / (scale[:, None] * scale[None, :])
    gain = (rounded * exact.conj()).sum(1).real / N
    g = np.block([[re, -im], [im, re]])
    after = 1 / (scale * gain * math.sqrt(N))
    before = 1 / scale
    outer = [np.outer(v, v) for v in (after * before, after, before, 1 / after)]
    return np.stack([g, g.T]), np.stack(outer).astype(np.float32)


TABLES, FACTORS = dft_tables()


def blocks(y):
    return y[:N, :N], y[:N, N:], y[N:, :N], y[N:, N:]


def square(a, b, c, d):
    return jnp.concatenate([jnp.concatenate([a, b], 1), jnp.concatenate([c, d], 1)], 0)


def swap(y):
    a, b, c, d = blocks(y)
    return square(a, c, b, d)


def dot(a, b):
    return jnp.dot(a, b, preferred_element_type=jnp.float32)


def left(tab, which, x):
    x = x.astype(jnp.bfloat16)
    return jnp.concatenate([dot(tab[which, :N], x), dot(tab[which, N:], x)], 0)


def right(tab, which, x):
    x = x.astype(jnp.bfloat16)
    return jnp.concatenate([dot(x[:N], tab[which]), dot(x[N:], tab[which])], 0)


def mul_columns(x, sr, si):
    r1, r2, i1, i2 = blocks(x)
    return square(sr * r1 - si * i1, sr * r2 - si * i2, sr * i1 + si * r1, sr * i2 + si * r2)


def mul_rows(x, sr, si):
    r1, i1, r2, i2 = blocks(x)
    return square(sr * r1 - si * i1, sr * i1 + si * r1, sr * r2 - si * i2, sr * i2 + si * r2)


def propagate(tab, xs, hr, hi):
    xs = [swap(left(tab, 0, x)) for x in xs]
    xs = [mul_rows(right(tab, 1, x), hr, hi) for x in xs]
    xs = [swap(right(tab, 0, x)) for x in xs]
    return [left(tab, 1, x) for x in xs]


def kernel(
    depth, tiles, slots, pairs,
    own_hbm, probe_hbm, phase_hbm, measured_hbm, counts, offsets, tab_hbm, fac_hbm,
    out,
    own, probe, phase, measured, tab, fac,
    frame, rows_of, cols_of, rows_back, cols_back, cropped, patch, screens, wave, prop, gout, gin, gcols, gframe,
    hout, hin, vout, vin,
    own_sem, in_sem, ring_sem,
    v_send, v_recv, h_send, h_recv, p_send, p_recv, g_send, g_recv, fh_send, fh_recv, fv_send, fv_recv,
):
    y = lax.axis_index("depth")
    t = lax.axis_index("tile")
    core = lax.rem(t, 2)
    col = lax.rem(t, TCOLS)
    row = lax.div(t, TCOLS)
    has_up, has_down = row > 0, row < tiles // TCOLS - 1
    has_left, has_right = col > 0, col < TCOLS - 1
    bf = jnp.bfloat16
    f32 = jnp.float32

    def worker(p):
        return WORKERS[0][p] + core * (WORKERS[1][p] - WORKERS[0][p])

    def load_own(ri, half):
        part = (ri, slice(half * N, (half + 1) * N))
        return pltpu.make_async_copy(own_hbm.at[part], own.at[part], own_sem.at[ri, half])

    def load(k):
        src, dst = ((phase_hbm, phase), (probe_hbm, probe), (tab_hbm, tab), (measured_hbm, measured), (fac_hbm, fac))[k]
        return pltpu.make_async_copy(src, dst, in_sem.at[k])

    for ri in range(2):
        for half in range(2):
            load_own(ri, half).start()

    barrier = pltpu.get_barrier_semaphore()
    around = ((has_up, -TCOLS), (has_down, TCOLS), (has_left, -1), (has_right, 1))
    for there, by in around:
        @pl.when(there)
        def _():
            pl.semaphore_signal(barrier, inc=1, device_id=(y, t + by), device_id_type=MESH)
    both_ways = (lax.rem(y + 1, depth), lax.rem(y + depth - 1, depth))
    for beside in both_ways:
        pl.semaphore_signal(barrier, inc=1, device_id=(beside, t), device_id_type=MESH)

    for k in range(5):
        load(k).start()

    def outside(ri, shape):
        return jnp.full(shape, -1.0 if ri == 0 else 0.0, bf)


    @pl.when(jnp.logical_not(has_up))
    def _():
        for ri in range(2):
            frame[ri, 1:3, 0:N] = outside(ri, (2, N, N))

    @pl.when(jnp.logical_not(has_down))
    def _():
        for ri in range(2):
            frame[ri, 1:3, 3 * N : 4 * N] = outside(ri, (2, N, N))

    @pl.when(jnp.logical_not(has_left))
    def _():
        for ri in range(2):
            frame[ri, 0] = outside(ri, (4 * N, N))

    @pl.when(jnp.logical_not(has_right))
    def _():
        for ri in range(2):
            frame[ri, 3] = outside(ri, (4 * N, N))

    for ri in range(2):
        for half in range(2):
            load_own(ri, half).wait()
            for cb in range(2):
                got = own[ri, half * N : (half + 1) * N, cb * N : (cb + 1) * N]
                frame[ri, 1 + cb, (1 + half) * N : (2 + half) * N] = (got - 1.0 if ri == 0 else got).astype(bf)

    pl.semaphore_wait(
        barrier,
        2 + sum(there.astype(jnp.int32) for there, _ in around),
    )

    rounds = depth // 2 - 1

    def hear_further(k):
        if 0 < k <= rounds:
            pl.semaphore_wait(ring_sem.at[k - 1], 2)
        if k < rounds:
            for beside in both_ways:
                pl.semaphore_signal(ring_sem.at[k], inc=1, device_id=(beside, t), device_id_type=MESH)

    def halo_down(ri):
        return pltpu.make_async_remote_copy(
            src_ref=frame.at[ri, 1:3, 2 * N : 3 * N], dst_ref=frame.at[ri, 1:3, 0:N],
            send_sem=v_send.at[0, ri], recv_sem=v_recv.at[0, ri], device_id=(y, t + TCOLS), device_id_type=MESH)

    def halo_up(ri):
        return pltpu.make_async_remote_copy(
            src_ref=frame.at[ri, 1:3, N : 2 * N], dst_ref=frame.at[ri, 1:3, 3 * N : 4 * N],
            send_sem=v_send.at[1, ri], recv_sem=v_recv.at[1, ri], device_id=(y, t - TCOLS), device_id_type=MESH)

    pieces = ((0, N), (3 * N, 4 * N), (N, 3 * N))

    def halo_right(ri, k):
        lo, hi = pieces[k]
        return pltpu.make_async_remote_copy(
            src_ref=frame.at[ri, 2, lo:hi], dst_ref=frame.at[ri, 0, lo:hi],
            send_sem=h_send.at[0, ri, k], recv_sem=h_recv.at[0, ri, k], device_id=(y, t + 1), device_id_type=MESH)

    def halo_left(ri, k):
        lo, hi = pieces[k]
        return pltpu.make_async_remote_copy(
            src_ref=frame.at[ri, 1, lo:hi], dst_ref=frame.at[ri, 3, lo:hi],
            send_sem=h_send.at[1, ri, k], recv_sem=h_recv.at[1, ri, k], device_id=(y, t - 1), device_id_type=MESH)

    def sideways(ri, k):
        @pl.when(has_right)
        def _():
            halo_right(ri, k).start()

        @pl.when(has_left)
        def _():
            halo_left(ri, k).start()

    def send_halo(ri):
        @pl.when(has_down)
        def _():
            halo_down(ri).start()

        @pl.when(has_up)
        def _():
            halo_up(ri).start()

        sideways(ri, 2)

    send_halo(0)
    hear_further(0)

    for p in range(slots):
        r, c = offsets[0, p], offsets[1, p]
        wide = lax.broadcasted_iota(jnp.int32, (N, 4 * N), 1) - lax.broadcasted_iota(jnp.int32, (N, 4 * N), 0)
        tall = lax.broadcasted_iota(jnp.int32, (4 * N, N), 0) - lax.broadcasted_iota(jnp.int32, (4 * N, N), 1)
        rows_of[p * N : (p + 1) * N] = jnp.where(wide == r, 1.0, 0.0).astype(bf)
        cols_back[p] = jnp.where(wide == c, 1.0, 0.0).astype(bf)
        rows_back[:, p * N : (p + 1) * N] = jnp.where(tall == r, 1.0, 0.0).astype(bf)
        cols_of[p] = jnp.where(tall == c, 1.0, 0.0).astype(bf)
    load(0).wait()
    angle = phase[...]
    hr, hi = jnp.cos(angle), jnp.sin(angle)
    load(4).wait()
    prop[0] = hr * fac[0]
    prop[1] = hi * fac[0]
    prop[2] = hr * fac[1]
    prop[3] = hi * fac[1]
    prop[4] = hr * fac[2]
    prop[5] = hi * fac[2]
    load(1).wait()
    for q in range(pairs):
        one, two = probe[2 * q], probe[2 * q + 1]
        wave[0, q] = square(one[0] * fac[3], two[0] * fac[3], one[1] * fac[3], two[1] * fac[3])
    load(2).wait()
    load(3).wait()
    hear_further(1)

    def crop_rows(ri, one, other):
        got = dot(rows_of[...], jnp.concatenate([frame[ri, one], frame[ri, other]], 1)).astype(bf)
        for p in range(slots):
            cropped[ri, p, :, one * N : (one + 1) * N] = got[p * N : (p + 1) * N, :N]
            cropped[ri, p, :, other * N : (other + 1) * N] = got[p * N : (p + 1) * N, N:]

    def patch_copy(p, s, ri):
        return pltpu.make_async_remote_copy(
            src_ref=patch.at[p, ri], dst_ref=screens.at[s, ri],
            send_sem=p_send.at[p, ri], recv_sem=p_recv.at[s, ri], device_id=(worker(p), t), device_id_type=MESH)

    def take_rows(ri):
        @pl.when(has_up)
        def _():
            halo_down(ri).wait_recv()

        sideways(ri, 0)

        @pl.when(has_down)
        def _():
            halo_up(ri).wait_recv()

        sideways(ri, 1)

    take_rows(0)
    send_halo(1)
    hear_further(2)
    for ri in range(2):
        if ri == 1:
            take_rows(1)
        crop_rows(ri, 1, 2)
        if ri == 0:
            hear_further(3)
        for k in (2, 0, 1):
            @pl.when(has_left)
            def _():
                halo_right(ri, k).wait_recv()

            @pl.when(has_right)
            def _():
                halo_left(ri, k).wait_recv()

        crop_rows(ri, 0, 3)
        for p in range(slots):
            patch[p, ri] = dot(cropped[ri, p], cols_of[p]).astype(bf)

        for p in range(slots):
            @pl.when(y != worker(p))
            def _():
                patch_copy(p, y, ri).start()

            @pl.when(y == worker(p))
            def _():
                screens[y, ri] = patch[p, ri]

    mine = sum(p * (y == worker(p)).astype(jnp.int32) for p in range(slots))
    working = sum((y == worker(p)).astype(jnp.int32) for p in range(slots)) > 0

    def grad_copy(s, p, ri):
        return pltpu.make_async_remote_copy(
            src_ref=gout.at[s, ri], dst_ref=gin.at[p, ri],
            send_sem=g_send.at[s, ri], recv_sem=g_recv.at[p, ri], device_id=(s, t), device_id_type=MESH)

    @pl.when(working)
    def _():
        def screen(s):
            return (screens[s, 0].astype(f32) + 1.0) * fac[0], screens[s, 1].astype(f32) * fac[0]

        def arrive(s):
            @pl.when(y != s)
            def _():
                for ri in range(2):
                    patch_copy(0, s, ri).wait_recv()

        def forward(s, carry):
            arrive(s)
            sr, si = screen(s)
            xs = [mul_columns(wave[s, q], sr, si) for q in range(pairs)]
            xs = propagate(tab, xs, prop[0], prop[1])
            for q in range(pairs):
                wave[s + 1, q] = xs[q]
            return carry

        lax.fori_loop(0, depth - 1, forward, 0)
        arrive(depth - 1)
        sr, si = screen(depth - 1)
        xs = [mul_columns(wave[depth - 1, q], sr, si) for q in range(pairs)]
        xs = [swap(left(tab, 0, x)) for x in xs]
        xs = [mul_rows(right(tab, 1, x), prop[2], prop[3]) for x in xs]
        intensity = jnp.zeros((N, N), f32)
        for x in xs:
            for part in blocks(x):
                intensity = intensity + part * part
        valid = jnp.where(mine < counts[0], 4.0, 0.0)
        weight = (intensity - measured[mine]) * valid
        xs = [mul_rows(x, prop[4] * weight, -prop[5] * weight) for x in xs]
        xs = [swap(right(tab, 0, x)) for x in xs]
        us = [left(tab, 1, x) for x in xs]

        for q in range(pairs):
            wave[depth, q] = us[q]

        def gradient(s, us):
            gr = jnp.zeros((N, N), f32)
            gi = jnp.zeros((N, N), f32)
            for q in range(pairs):
                u, v = blocks(us[q]), blocks(wave[s, q])
                for k in range(2):
                    gr = gr + u[k] * v[k] + u[2 + k] * v[2 + k]
                    gi = gi + u[2 + k] * v[k] - u[k] * v[2 + k]
            back = fac[1] * fac[1]
            gout[s, 0] = (gr * back).astype(bf)
            gout[s, 1] = (gi * back).astype(bf)

        def leave(s):
            @pl.when(y != s)
            def _():
                for ri in range(2):
                    grad_copy(s, mine, ri).start()

            @pl.when(y == s)
            def _():
                gin[mine] = gout[s]

        def backward(k, carry):
            s = depth - 1 - k
            us = [wave[depth, q] for q in range(pairs)]
            sr, si = screen(s)
            xs = propagate(tab, [mul_columns(u, sr, -si) for u in us], prop[0], -prop[1])
            gradient(s, us)
            for q in range(pairs):
                wave[depth, q] = xs[q]
            leave(s)
            return carry

        lax.fori_loop(0, depth - 1, backward, 0)
        gradient(0, [wave[depth, q] for q in range(pairs)])
        leave(0)

    def fold_left(ri, k):
        lo, hi = pieces[k]
        return pltpu.make_async_remote_copy(
            src_ref=hout.at[0, ri, lo:hi], dst_ref=hin.at[0, ri, lo:hi],
            send_sem=fh_send.at[0, ri, k], recv_sem=fh_recv.at[0, ri, k], device_id=(y, t - 1), device_id_type=MESH)

    def fold_right(ri, k):
        lo, hi = pieces[k]
        return pltpu.make_async_remote_copy(
            src_ref=hout.at[1, ri, lo:hi], dst_ref=hin.at[1, ri, lo:hi],
            send_sem=fh_send.at[1, ri, k], recv_sem=fh_recv.at[1, ri, k], device_id=(y, t + 1), device_id_type=MESH)

    def send_sides(ri, k):
        @pl.when(has_left)
        def _():
            fold_left(ri, k).start()

        @pl.when(has_right)
        def _():
            fold_right(ri, k).start()

    for ri in range(2):
        for p in range(slots):
            @pl.when(y != worker(p))
            def _():
                grad_copy(0, p, ri).wait_recv()

        for p in range(slots):
            got = dot(gin[p, ri], cols_back[p]).astype(bf)
            for cb in range(4):
                at = (0, 2, 3, 1)[cb]
                gcols[ri, p * N : (p + 1) * N, at * N : (at + 1) * N] = got[:, cb * N : (cb + 1) * N]
        got = dot(rows_back[...], gcols[ri, :, : 2 * N]).astype(bf)
        hout[0, ri] = got[:, :N]
        hout[1, ri] = got[:, N:]
        send_sides(ri, 0)
        send_sides(ri, 1)
        got = dot(rows_back[...], gcols[ri, :, 2 * N :])
        gframe[ri, 0] = got[:, :N]
        gframe[ri, 1] = got[:, N:]

    def fold_up(ri):
        return pltpu.make_async_remote_copy(
            src_ref=vout.at[0, ri], dst_ref=vin.at[0, ri],
            send_sem=fv_send.at[0, ri], recv_sem=fv_recv.at[0, ri], device_id=(y, t - TCOLS), device_id_type=MESH)

    def fold_down(ri):
        return pltpu.make_async_remote_copy(
            src_ref=vout.at[1, ri], dst_ref=vin.at[1, ri],
            send_sem=fv_send.at[1, ri], recv_sem=fv_recv.at[1, ri], device_id=(y, t + TCOLS), device_id_type=MESH)

    def take_sides(ri, k):
        lo, hi = pieces[k]

        @pl.when(has_right)
        def _():
            fold_left(ri, k).wait_recv()
            gframe[ri, 1, lo:hi] = gframe[ri, 1, lo:hi] + hin[0, ri, lo:hi].astype(f32)

        @pl.when(has_left)
        def _():
            fold_right(ri, k).wait_recv()
            gframe[ri, 0, lo:hi] = gframe[ri, 0, lo:hi] + hin[1, ri, lo:hi].astype(f32)

    for ri in range(2):
        take_sides(ri, 0)
        vout[0, ri] = gframe[ri, :, 0:N].astype(bf)

        @pl.when(has_up)
        def _():
            fold_up(ri).start()

        take_sides(ri, 1)
        vout[1, ri] = gframe[ri, :, 3 * N : 4 * N].astype(bf)

        @pl.when(has_down)
        def _():
            fold_down(ri).start()

        send_sides(ri, 2)

    for ri in range(2):
        take_sides(ri, 2)
        for cb in range(2):
            out[ri, :, cb * N : (cb + 1) * N] = gframe[ri, cb, N : 3 * N]

    for ri in range(2):
        @pl.when(has_up)
        def _():
            fold_down(ri).wait_recv()
            for cb in range(2):
                at = (ri, slice(0, N), slice(cb * N, (cb + 1) * N))
                out[at] = out[at] + vin[1, ri, cb].astype(f32)

        @pl.when(has_down)
        def _():
            fold_up(ri).wait_recv()
            for cb in range(2):
                at = (ri, slice(N, 2 * N), slice(cb * N, (cb + 1) * N))
                out[at] = out[at] + vin[0, ri, cb].astype(f32)

    for ri in range(2):
        @pl.when(has_down)
        def _():
            halo_down(ri).wait_send()
            fold_down(ri).wait_send()

        @pl.when(has_up)
        def _():
            halo_up(ri).wait_send()
            fold_up(ri).wait_send()

        @pl.when(has_right)
        def _():
            for k in range(3):
                halo_right(ri, k).wait_send()
                fold_right(ri, k).wait_send()

        @pl.when(has_left)
        def _():
            for k in range(3):
                halo_left(ri, k).wait_send()
                fold_left(ri, k).wait_send()

        for p in range(slots):
            @pl.when(y != worker(p))
            def _():
                patch_copy(p, 0, ri).wait_send()

    for s in range(depth):
        @pl.when(jnp.logical_and(working, y != s))
        def _():
            for ri in range(2):
                grad_copy(s, 0, ri).wait_send()


def body(depth, tiles, transmission, probe_modes, propagator_phase, measured, counts, offsets):
    slots = offsets.shape[1]
    pairs = probe_modes.shape[0] // 2
    bf, f32 = jnp.bfloat16, jnp.float32
    vmem = pl.BlockSpec(memory_space=pltpu.VMEM)
    hbm = pl.BlockSpec(memory_space=pl.ANY)
    smem = pl.BlockSpec(memory_space=pltpu.SMEM)
    dma = pltpu.SemaphoreType.DMA
    grad = pl.pallas_call(
        functools.partial(kernel, depth, tiles, slots, pairs),
        out_shape=pltpu.VMEM((2, 2 * N, 2 * N), f32),
        in_specs=[hbm, hbm, hbm, hbm, smem, smem, hbm, hbm],
        out_specs=vmem,
        scratch_shapes=[
            pltpu.VMEM((2, 2 * N, 2 * N), f32),
            pltpu.VMEM(probe_modes.shape, f32),
            pltpu.VMEM((N, N), f32),
            pltpu.VMEM((slots, N, N), f32),
            pltpu.VMEM(TABLES.shape, bf),
            pltpu.VMEM(FACTORS.shape, f32),
            pltpu.VMEM((2, 4, 4 * N, N), bf),
            pltpu.VMEM((slots * N, 4 * N), bf),
            pltpu.VMEM((slots, 4 * N, N), bf),
            pltpu.VMEM((4 * N, slots * N), bf),
            pltpu.VMEM((slots, N, 4 * N), bf),
            pltpu.VMEM((2, slots, N, 4 * N), bf),
            pltpu.VMEM((slots, 2, N, N), bf),
            pltpu.VMEM((depth, 2, N, N), bf),
            pltpu.VMEM((depth + 1, pairs, 2 * N, 2 * N), f32),
            pltpu.VMEM((6, N, N), f32),
            pltpu.VMEM((depth, 2, N, N), bf),
            pltpu.VMEM((slots, 2, N, N), bf),
            pltpu.VMEM((2, slots * N, 4 * N), bf),
            pltpu.VMEM((2, 2, 4 * N, N), f32),
            pltpu.VMEM((2, 2, 4 * N, N), bf),
            pltpu.VMEM((2, 2, 4 * N, N), bf),
            pltpu.VMEM((2, 2, 2, N, N), bf),
            pltpu.VMEM((2, 2, 2, N, N), bf),
            dma((2, 2)), dma((5,)), pltpu.SemaphoreType.REGULAR((max(1, depth // 2 - 1),)),
            dma((2, 2)), dma((2, 2)), dma((2, 2, 3)), dma((2, 2, 3)),
            dma((slots, 2)), dma((depth, 2)), dma((depth, 2)), dma((slots, 2)),
            dma((2, 2, 3)), dma((2, 2, 3)), dma((2, 2)), dma((2, 2)),
        ],
        compiler_params=pltpu.CompilerParams(
            collective_id=0, has_side_effects=True, vmem_limit_bytes=56 * 2**20
        ),
        cost_estimate=pl.CostEstimate(flops=2 * 10**10, bytes_accessed=3 * 2**20, transcendentals=2 * N * N),
    )(
        transmission[0, 0], probe_modes, propagator_phase, measured[0], counts, jnp.transpose(offsets[0]),
        jnp.asarray(TABLES), jnp.asarray(FACTORS),
    )
    return grad[None, None]


def solution(mesh):
    return jax.shard_map(
        functools.partial(body, mesh.shape["depth"], mesh.shape["tile"]),
        mesh=mesh,
        in_specs=(
            P("depth", "tile", None, None, None),
            P(),
            P(),
            P("tile", None, None, None),
            P("tile"),
            P("tile", None, None),
        ),
        out_specs=P("depth", "tile", None, None, None),
        check_vma=False,
    )
```

```python
import functools
import math

import jax
import jax.numpy as jnp
import ml_dtypes
import numpy as np
from jax import lax
from jax.experimental import pallas as pl
from jax.experimental.pallas import tpu as pltpu
from jax.sharding import PartitionSpec as P

TCOLS = 4
N = 128
WORKERS = ((0, 1, 3, 6), (1, 2, 5, 7))
MESH = pl.DeviceIdType.MESH
CLASS_SCALES = 1.2742026, 1.2925407, 1.5548331, 1.5449858, 1.3945649, 1.3043629, 1.3043644, 1.3043595


def dft_tables():
    k = np.arange(N)
    scale = np.array([CLASS_SCALES[-1 if j == 0 else (j & -j).bit_length() - 1] for j in range(N)])
    angle = -2 * np.pi * ((k[:, None] * k[None, :]) % N) / N
    exact = np.exp(1j * angle)
    held = exact * scale[:, None] * scale[None, :]
    re, im = held.real.astype(np.float32).astype(ml_dtypes.bfloat16), held.imag.astype(np.float32).astype(ml_dtypes.bfloat16)
    rounded = (re.astype(np.float64) + 1j * im.astype(np.float64)) / (scale[:, None] * scale[None, :])
    gain = (rounded * exact.conj()).sum(1).real / N
    g = np.block([[re, -im], [im, re]])
    after = 1 / (scale * gain * math.sqrt(N))
    before = 1 / scale
    outer = [np.outer(v, v) for v in (after * before, after, before, 1 / after)]
    return np.stack([g, g.T]), np.stack(outer).astype(np.float32)


TABLES, FACTORS = dft_tables()


def blocks(y):
    return y[:N, :N], y[:N, N:], y[N:, :N], y[N:, N:]


def square(a, b, c, d):
    return jnp.concatenate([jnp.concatenate([a, b], 1), jnp.concatenate([c, d], 1)], 0)


def swap(y):
    a, b, c, d = blocks(y)
    return square(a, c, b, d)


def dot(a, b):
    return jnp.dot(a, b, preferred_element_type=jnp.float32)


def left(tab, which, x):
    x = x.astype(jnp.bfloat16)
    return jnp.concatenate([dot(tab[which, :N], x), dot(tab[which, N:], x)], 0)


def right(tab, which, x):
    x = x.astype(jnp.bfloat16)
    return jnp.concatenate([dot(x[:N], tab[which]), dot(x[N:], tab[which])], 0)


def mul_columns(x, sr, si):
    r1, r2, i1, i2 = blocks(x)
    return square(sr * r1 - si * i1, sr * r2 - si * i2, sr * i1 + si * r1, sr * i2 + si * r2)


def mul_rows(x, sr, si):
    r1, i1, r2, i2 = blocks(x)
    return square(sr * r1 - si * i1, sr * i1 + si * r1, sr * r2 - si * i2, sr * i2 + si * r2)


def propagate(tab, xs, hr, hi):
    xs = [swap(left(tab, 0, x)) for x in xs]
    xs = [mul_rows(right(tab, 1, x), hr, hi) for x in xs]
    xs = [swap(right(tab, 0, x)) for x in xs]
    return [left(tab, 1, x) for x in xs]


def kernel(
    depth, tiles, slots, pairs,
    own_hbm, probe_hbm, phase_hbm, measured_hbm, counts, offsets, tab_hbm, fac_hbm,
    out,
    own, probe, phase, measured, tab, fac,
    frame, rows_of, cols_of, rows_back, cols_back, cropped, patch, screens, wave, prop, gout, gin, gcols, gframe,
    hout, hin, vout, vin,
    own_sem, in_sem, ring_sem,
    v_send, v_recv, h_send, h_recv, p_send, p_recv, g_send, g_recv, fh_send, fh_recv, fv_send, fv_recv,
):
    y = lax.axis_index("depth")
    t = lax.axis_index("tile")
    core = lax.rem(t, 2)
    col = lax.rem(t, TCOLS)
    row = lax.div(t, TCOLS)
    has_up, has_down = row > 0, row < tiles // TCOLS - 1
    has_left, has_right = col > 0, col < TCOLS - 1
    bf = jnp.bfloat16
    f32 = jnp.float32

    def worker(p):
        return WORKERS[0][p] + core * (WORKERS[1][p] - WORKERS[0][p])

    def load_own(ri, half):
        part = (ri, slice(half * N, (half + 1) * N))
        return pltpu.make_async_copy(own_hbm.at[part], own.at[part], own_sem.at[ri, half])

    def load(k):
        src, dst = ((phase_hbm, phase), (probe_hbm, probe), (tab_hbm, tab), (measured_hbm, measured), (fac_hbm, fac))[k]
        return pltpu.make_async_copy(src, dst, in_sem.at[k])

    for ri in range(2):
        for half in range(2):
            load_own(ri, half).start()

    barrier = pltpu.get_barrier_semaphore()
    around = ((has_up, -TCOLS), (has_down, TCOLS), (has_left, -1), (has_right, 1))
    for there, by in around:
        @pl.when(there)
        def _():
            pl.semaphore_signal(barrier, inc=1, device_id=(y, t + by), device_id_type=MESH)
    both_ways = (lax.rem(y + 1, depth), lax.rem(y + depth - 1, depth))
    for beside in both_ways:
        pl.semaphore_signal(barrier, inc=1, device_id=(beside, t), device_id_type=MESH)

    for k in range(5):
        load(k).start()

    def outside(ri, shape):
        return jnp.full(shape, -1.0 if ri == 0 else 0.0, bf)


    @pl.when(jnp.logical_not(has_up))
    def _():
        for ri in range(2):
            frame[ri, 1:3, 0:N] = outside(ri, (2, N, N))

    @pl.when(jnp.logical_not(has_down))
    def _():
        for ri in range(2):
            frame[ri, 1:3, 3 * N : 4 * N] = outside(ri, (2, N, N))

    @pl.when(jnp.logical_not(has_left))
    def _():
        for ri in range(2):
            frame[ri, 0] = outside(ri, (4 * N, N))

    @pl.when(jnp.logical_not(has_right))
    def _():
        for ri in range(2):
            frame[ri, 3] = outside(ri, (4 * N, N))

    def fill(ri):
        for half in range(2):
            load_own(ri, half).wait()
            for cb in range(2):
                got = own[ri, half * N : (half + 1) * N, cb * N : (cb + 1) * N]
                frame[ri, 1 + cb, (1 + half) * N : (2 + half) * N] = (got - 1.0 if ri == 0 else got).astype(bf)

    fill(0)

    pl.semaphore_wait(
        barrier,
        2 + sum(there.astype(jnp.int32) for there, _ in around),
    )

    rounds = depth // 2 - 1

    def hear_further(k):
        if 0 < k <= rounds:
            pl.semaphore_wait(ring_sem.at[k - 1], 2)
        if k < rounds:
            for beside in both_ways:
                pl.semaphore_signal(ring_sem.at[k], inc=1, device_id=(beside, t), device_id_type=MESH)

    def halo_down(ri):
        return pltpu.make_async_remote_copy(
            src_ref=frame.at[ri, 1:3, 2 * N : 3 * N], dst_ref=frame.at[ri, 1:3, 0:N],
            send_sem=v_send.at[0, ri], recv_sem=v_recv.at[0, ri], device_id=(y, t + TCOLS), device_id_type=MESH)

    def halo_up(ri):
        return pltpu.make_async_remote_copy(
            src_ref=frame.at[ri, 1:3, N : 2 * N], dst_ref=frame.at[ri, 1:3, 3 * N : 4 * N],
            send_sem=v_send.at[1, ri], recv_sem=v_recv.at[1, ri], device_id=(y, t - TCOLS), device_id_type=MESH)

    pieces = ((0, N), (3 * N, 4 * N), (N, 3 * N))

    def halo_right(ri, k):
        lo, hi = pieces[k]
        return pltpu.make_async_remote_copy(
            src_ref=frame.at[ri, 2, lo:hi], dst_ref=frame.at[ri, 0, lo:hi],
            send_sem=h_send.at[0, ri, k], recv_sem=h_recv.at[0, ri, k], device_id=(y, t + 1), device_id_type=MESH)

    def halo_left(ri, k):
        lo, hi = pieces[k]
        return pltpu.make_async_remote_copy(
            src_ref=frame.at[ri, 1, lo:hi], dst_ref=frame.at[ri, 3, lo:hi],
            send_sem=h_send.at[1, ri, k], recv_sem=h_recv.at[1, ri, k], device_id=(y, t - 1), device_id_type=MESH)

    def sideways(ri, k):
        @pl.when(has_right)
        def _():
            halo_right(ri, k).start()

        @pl.when(has_left)
        def _():
            halo_left(ri, k).start()

    def send_halo(ri):
        @pl.when(has_down)
        def _():
            halo_down(ri).start()

        @pl.when(has_up)
        def _():
            halo_up(ri).start()

        sideways(ri, 2)

    send_halo(0)
    hear_further(0)
    fill(1)

    for p in range(slots):
        r, c = offsets[0, p], offsets[1, p]
        wide = lax.broadcasted_iota(jnp.int32, (N, 4 * N), 1) - lax.broadcasted_iota(jnp.int32, (N, 4 * N), 0)
        tall = lax.broadcasted_iota(jnp.int32, (4 * N, N), 0) - lax.broadcasted_iota(jnp.int32, (4 * N, N), 1)
        rows_of[p * N : (p + 1) * N] = jnp.where(wide == r, 1.0, 0.0).astype(bf)
        cols_back[p] = jnp.where(wide == c, 1.0, 0.0).astype(bf)
        rows_back[:, p * N : (p + 1) * N] = jnp.where(tall == r, 1.0, 0.0).astype(bf)
        cols_of[p] = jnp.where(tall == c, 1.0, 0.0).astype(bf)
    load(0).wait()
    angle = phase[...]
    hr, hi = jnp.cos(angle), jnp.sin(angle)
    load(4).wait()
    prop[0] = hr * fac[0]
    prop[1] = hi * fac[0]
    prop[2] = hr * fac[1]
    prop[3] = hi * fac[1]
    prop[4] = hr * fac[2]
    prop[5] = hi * fac[2]
    load(1).wait()
    for q in range(pairs):
        one, two = probe[2 * q], probe[2 * q + 1]
        wave[0, q] = square(one[0] * fac[3], two[0] * fac[3], one[1] * fac[3], two[1] * fac[3])
    load(2).wait()
    load(3).wait()
    hear_further(1)

    def crop_rows(ri, one, other):
        got = dot(rows_of[...], jnp.concatenate([frame[ri, one], frame[ri, other]], 1)).astype(bf)
        for p in range(slots):
            cropped[ri, p, :, one * N : (one + 1) * N] = got[p * N : (p + 1) * N, :N]
            cropped[ri, p, :, other * N : (other + 1) * N] = got[p * N : (p + 1) * N, N:]

    def patch_copy(p, s, ri):
        return pltpu.make_async_remote_copy(
            src_ref=patch.at[p, ri], dst_ref=screens.at[s, ri],
            send_sem=p_send.at[p, ri], recv_sem=p_recv.at[s, ri], device_id=(worker(p), t), device_id_type=MESH)

    def take_rows(ri):
        @pl.when(has_up)
        def _():
            halo_down(ri).wait_recv()

        sideways(ri, 0)

        @pl.when(has_down)
        def _():
            halo_up(ri).wait_recv()

        sideways(ri, 1)

    take_rows(0)
    send_halo(1)
    hear_further(2)
    for ri in range(2):
        if ri == 1:
            take_rows(1)
        crop_rows(ri, 1, 2)
        if ri == 0:
            hear_further(3)
        for k in (2, 0, 1):
            @pl.when(has_left)
            def _():
                halo_right(ri, k).wait_recv()

            @pl.when(has_right)
            def _():
                halo_left(ri, k).wait_recv()

        crop_rows(ri, 0, 3)
        for p in range(slots):
            patch[p, ri] = dot(cropped[ri, p], cols_of[p]).astype(bf)

        for p in range(slots):
            @pl.when(y != worker(p))
            def _():
                patch_copy(p, y, ri).start()

            @pl.when(y == worker(p))
            def _():
                screens[y, ri] = patch[p, ri]

    mine = sum(p * (y == worker(p)).astype(jnp.int32) for p in range(slots))
    working = sum((y == worker(p)).astype(jnp.int32) for p in range(slots)) > 0

    def grad_copy(s, p, ri):
        return pltpu.make_async_remote_copy(
            src_ref=gout.at[s, ri], dst_ref=gin.at[p, ri],
            send_sem=g_send.at[s, ri], recv_sem=g_recv.at[p, ri], device_id=(s, t), device_id_type=MESH)

    @pl.when(working)
    def _():
        def screen(s):
            return (screens[s, 0].astype(f32) + 1.0) * fac[0], screens[s, 1].astype(f32) * fac[0]

        def arrive(s):
            @pl.when(y != s)
            def _():
                for ri in range(2):
                    patch_copy(0, s, ri).wait_recv()

        def forward(s, carry):
            arrive(s)
            sr, si = screen(s)
            xs = [mul_columns(wave[s, q], sr, si) for q in range(pairs)]
            xs = propagate(tab, xs, prop[0], prop[1])
            for q in range(pairs):
                wave[s + 1, q] = xs[q]
            return carry

        lax.fori_loop(0, depth - 1, forward, 0)
        arrive(depth - 1)
        sr, si = screen(depth - 1)
        xs = [mul_columns(wave[depth - 1, q], sr, si) for q in range(pairs)]
        xs = [swap(left(tab, 0, x)) for x in xs]
        xs = [mul_rows(right(tab, 1, x), prop[2], prop[3]) for x in xs]
        intensity = jnp.zeros((N, N), f32)
        for x in xs:
            for part in blocks(x):
                intensity = intensity + part * part
        valid = jnp.where(mine < counts[0], 4.0, 0.0)
        weight = (intensity - measured[mine]) * valid
        xs = [mul_rows(x, prop[4] * weight, -prop[5] * weight) for x in xs]
        xs = [swap(right(tab, 0, x)) for x in xs]
        us = [left(tab, 1, x) for x in xs]

        for q in range(pairs):
            wave[depth, q] = us[q]

        def gradient(s, us):
            gr = jnp.zeros((N, N), f32)
            gi = jnp.zeros((N, N), f32)
            for q in range(pairs):
                u, v = blocks(us[q]), blocks(wave[s, q])
                for k in range(2):
                    gr = gr + u[k] * v[k] + u[2 + k] * v[2 + k]
                    gi = gi + u[2 + k] * v[k] - u[k] * v[2 + k]
            back = fac[1] * fac[1]
            gout[s, 0] = (gr * back).astype(bf)
            gout[s, 1] = (gi * back).astype(bf)

        def leave(s):
            @pl.when(y != s)
            def _():
                for ri in range(2):
                    grad_copy(s, mine, ri).start()

            @pl.when(y == s)
            def _():
                gin[mine] = gout[s]

        def backward(k, carry):
            s = depth - 1 - k
            us = [wave[depth, q] for q in range(pairs)]
            sr, si = screen(s)
            xs = propagate(tab, [mul_columns(u, sr, -si) for u in us], prop[0], -prop[1])
            gradient(s, us)
            for q in range(pairs):
                wave[depth, q] = xs[q]
            leave(s)
            return carry

        lax.fori_loop(0, depth - 1, backward, 0)
        gradient(0, [wave[depth, q] for q in range(pairs)])
        leave(0)

    def fold_left(ri, k):
        lo, hi = pieces[k]
        return pltpu.make_async_remote_copy(
            src_ref=hout.at[0, ri, lo:hi], dst_ref=hin.at[0, ri, lo:hi],
            send_sem=fh_send.at[0, ri, k], recv_sem=fh_recv.at[0, ri, k], device_id=(y, t - 1), device_id_type=MESH)

    def fold_right(ri, k):
        lo, hi = pieces[k]
        return pltpu.make_async_remote_copy(
            src_ref=hout.at[1, ri, lo:hi], dst_ref=hin.at[1, ri, lo:hi],
            send_sem=fh_send.at[1, ri, k], recv_sem=fh_recv.at[1, ri, k], device_id=(y, t + 1), device_id_type=MESH)

    def send_sides(ri, k):
        @pl.when(has_left)
        def _():
            fold_left(ri, k).start()

        @pl.when(has_right)
        def _():
            fold_right(ri, k).start()

    for ri in range(2):
        for p in range(slots):
            @pl.when(y != worker(p))
            def _():
                grad_copy(0, p, ri).wait_recv()

        for p in range(slots):
            sides = jnp.concatenate([cols_back[p, :, :N], cols_back[p, :, 3 * N :]], 1)
            gcols[ri, p * N : (p + 1) * N, : 2 * N] = dot(gin[p, ri], sides).astype(bf)
        got = dot(rows_back[...], gcols[ri, :, : 2 * N]).astype(bf)
        hout[0, ri] = got[:, :N]
        hout[1, ri] = got[:, N:]
        send_sides(ri, 0)
        send_sides(ri, 1)
        for p in range(slots):
            gcols[ri, p * N : (p + 1) * N, 2 * N :] = dot(gin[p, ri], cols_back[p, :, N : 3 * N]).astype(bf)
        got = dot(rows_back[...], gcols[ri, :, 2 * N :])
        gframe[ri, 0] = got[:, :N]
        gframe[ri, 1] = got[:, N:]

    def fold_up(ri):
        return pltpu.make_async_remote_copy(
            src_ref=vout.at[0, ri], dst_ref=vin.at[0, ri],
            send_sem=fv_send.at[0, ri], recv_sem=fv_recv.at[0, ri], device_id=(y, t - TCOLS), device_id_type=MESH)

    def fold_down(ri):
        return pltpu.make_async_remote_copy(
            src_ref=vout.at[1, ri], dst_ref=vin.at[1, ri],
            send_sem=fv_send.at[1, ri], recv_sem=fv_recv.at[1, ri], device_id=(y, t + TCOLS), device_id_type=MESH)

    def take_sides(ri, k):
        lo, hi = pieces[k]

        @pl.when(has_right)
        def _():
            fold_left(ri, k).wait_recv()
            gframe[ri, 1, lo:hi] = gframe[ri, 1, lo:hi] + hin[0, ri, lo:hi].astype(f32)

        @pl.when(has_left)
        def _():
            fold_right(ri, k).wait_recv()
            gframe[ri, 0, lo:hi] = gframe[ri, 0, lo:hi] + hin[1, ri, lo:hi].astype(f32)

    for ri in range(2):
        take_sides(ri, 0)
        vout[0, ri] = gframe[ri, :, 0:N].astype(bf)

        @pl.when(has_up)
        def _():
            fold_up(ri).start()

        take_sides(ri, 1)
        vout[1, ri] = gframe[ri, :, 3 * N : 4 * N].astype(bf)

        @pl.when(has_down)
        def _():
            fold_down(ri).start()

        send_sides(ri, 2)

    for ri in range(2):
        take_sides(ri, 2)
        for cb in range(2):
            out[ri, :, cb * N : (cb + 1) * N] = gframe[ri, cb, N : 3 * N]

    for ri in range(2):
        @pl.when(has_up)
        def _():
            fold_down(ri).wait_recv()
            for cb in range(2):
                at = (ri, slice(0, N), slice(cb * N, (cb + 1) * N))
                out[at] = out[at] + vin[1, ri, cb].astype(f32)

        @pl.when(has_down)
        def _():
            fold_up(ri).wait_recv()
            for cb in range(2):
                at = (ri, slice(N, 2 * N), slice(cb * N, (cb + 1) * N))
                out[at] = out[at] + vin[0, ri, cb].astype(f32)

    for ri in range(2):
        @pl.when(has_down)
        def _():
            halo_down(ri).wait_send()
            fold_down(ri).wait_send()

        @pl.when(has_up)
        def _():
            halo_up(ri).wait_send()
            fold_up(ri).wait_send()

        @pl.when(has_right)
        def _():
            for k in range(3):
                halo_right(ri, k).wait_send()
                fold_right(ri, k).wait_send()

        @pl.when(has_left)
        def _():
            for k in range(3):
                halo_left(ri, k).wait_send()
                fold_left(ri, k).wait_send()

        for p in range(slots):
            @pl.when(y != worker(p))
            def _():
                patch_copy(p, 0, ri).wait_send()

    for s in range(depth):
        @pl.when(jnp.logical_and(working, y != s))
        def _():
            for ri in range(2):
                grad_copy(s, 0, ri).wait_send()


def body(depth, tiles, transmission, probe_modes, propagator_phase, measured, counts, offsets):
    slots = offsets.shape[1]
    pairs = probe_modes.shape[0] // 2
    bf, f32 = jnp.bfloat16, jnp.float32
    vmem = pl.BlockSpec(memory_space=pltpu.VMEM)
    hbm = pl.BlockSpec(memory_space=pl.ANY)
    smem = pl.BlockSpec(memory_space=pltpu.SMEM)
    dma = pltpu.SemaphoreType.DMA
    grad = pl.pallas_call(
        functools.partial(kernel, depth, tiles, slots, pairs),
        out_shape=pltpu.VMEM((2, 2 * N, 2 * N), f32),
        in_specs=[hbm, hbm, hbm, hbm, smem, smem, hbm, hbm],
        out_specs=vmem,
        scratch_shapes=[
            pltpu.VMEM((2, 2 * N, 2 * N), f32),
            pltpu.VMEM(probe_modes.shape, f32),
            pltpu.VMEM((N, N), f32),
            pltpu.VMEM((slots, N, N), f32),
            pltpu.VMEM(TABLES.shape, bf),
            pltpu.VMEM(FACTORS.shape, f32),
            pltpu.VMEM((2, 4, 4 * N, N), bf),
            pltpu.VMEM((slots * N, 4 * N), bf),
            pltpu.VMEM((slots, 4 * N, N), bf),
            pltpu.VMEM((4 * N, slots * N), bf),
            pltpu.VMEM((slots, N, 4 * N), bf),
            pltpu.VMEM((2, slots, N, 4 * N), bf),
            pltpu.VMEM((slots, 2, N, N), bf),
            pltpu.VMEM((depth, 2, N, N), bf),
            pltpu.VMEM((depth + 1, pairs, 2 * N, 2 * N), f32),
            pltpu.VMEM((6, N, N), f32),
            pltpu.VMEM((depth, 2, N, N), bf),
            pltpu.VMEM((slots, 2, N, N), bf),
            pltpu.VMEM((2, slots * N, 4 * N), bf),
            pltpu.VMEM((2, 2, 4 * N, N), f32),
            pltpu.VMEM((2, 2, 4 * N, N), bf),
            pltpu.VMEM((2, 2, 4 * N, N), bf),
            pltpu.VMEM((2, 2, 2, N, N), bf),
            pltpu.VMEM((2, 2, 2, N, N), bf),
            dma((2, 2)), dma((5,)), pltpu.SemaphoreType.REGULAR((max(1, depth // 2 - 1),)),
            dma((2, 2)), dma((2, 2)), dma((2, 2, 3)), dma((2, 2, 3)),
            dma((slots, 2)), dma((depth, 2)), dma((depth, 2)), dma((slots, 2)),
            dma((2, 2, 3)), dma((2, 2, 3)), dma((2, 2)), dma((2, 2)),
        ],
        compiler_params=pltpu.CompilerParams(
            collective_id=0, has_side_effects=True, vmem_limit_bytes=56 * 2**20
        ),
        cost_estimate=pl.CostEstimate(flops=2 * 10**10, bytes_accessed=3 * 2**20, transcendentals=2 * N * N),
    )(
        transmission[0, 0], probe_modes, propagator_phase, measured[0], counts, jnp.transpose(offsets[0]),
        jnp.asarray(TABLES), jnp.asarray(FACTORS),
    )
    return grad[None, None]


def solution(mesh):
    return jax.shard_map(
        functools.partial(body, mesh.shape["depth"], mesh.shape["tile"]),
        mesh=mesh,
        in_specs=(
            P("depth", "tile", None, None, None),
            P(),
            P(),
            P("tile", None, None, None),
            P("tile"),
            P("tile", None, None),
        ),
        out_specs=P("depth", "tile", None, None, None),
        check_vma=False,
    )
```
